32 devices in a mesh: parts: 2 (over x), bins: 8 (over z, y), pix: 2 (over core).
Axes of the slice: x: 2, y: 2, z: 4, core: 2. Of those that a mesh axis runs over, the one named last changes fastest.
Arguments:
- spectra: bfloat16 [16384, 8192], P(('parts', 'pix'), 'bins'), parts along dimension 0, may hold values from -45 to 45
- probes: bfloat16 [16384, 256], P(('parts', 'pix')), parts along dimension 0, may hold values from -6 to 6
Outputs:
- basis: float32 [4, 4096, 256], P(('parts', 'pix'), 'bins'), parts along dimension 0
The draws below stay inside these ranges and needn't reach their ends.
There are 2 independent parts, one for each index of `parts`. The reference program is written for one: setup_inputs(seed, part) draws one part's arguments, and reference() takes and returns one part's arrays. A program takes and returns all parts, laid end to end along the dimension named above; each array names one. Nothing has to cross between parts.
All inputs are finite; a program needn't handle non-finite values.
Results may differ from the reference program's by a relative error of at most 0.0025.
Values may be sent and summed in bfloat16 or wider, within the bound.
No kernel may reach another device: no remote copies, remote signals or barrier semaphores. Data moves between devices by JAX's collectives and lax.ppermute only.
A program may use at most 64 MiB of HBM per device.

```python
import math
import jax
import jax.numpy as jnp
from jax import lax

PIX_DEV = 4096
K = 256
PIXELS = 8192
BINS = 8192
N_PIX = 2


def draw_spectra(key, part):
    key = jax.random.fold_in(key, 11)
    key_base, key_rows, key_cols = jax.random.split(key, 3)
    row_scale = jnp.exp(jax.random.uniform(key_rows, (PIXELS, 1), jnp.float32) * math.log(10.0))
    col_scale = jnp.exp(jax.random.uniform(key_cols, (1, BINS), jnp.float32) * math.log(10.0))
    base = jax.random.truncated_normal(key_base, -4.0, 4.0, (PIXELS, BINS), jnp.float32)
    return (0.1 * row_scale * col_scale * base).astype(jnp.bfloat16)


def steps_of(stream_key, extent, pieces, least, top_value):
    loudness, own = 1.0, jax.random.fold_in(stream_key, 6)
    for dim, parts in pieces:
        heights = jnp.exp(jax.random.uniform(jax.random.fold_in(own, dim), (parts,), jnp.float32, least / len(pieces), top_value / len(pieces)))
        loudness = loudness * jnp.repeat(heights, extent[dim] // parts).reshape([-1 if axis == dim else 1 for axis in range(len(extent))])
    return loudness


def noise(own_key, dims, width, most, pieces=(), held_as=jnp.bfloat16):
    gain = steps_of(own_key, dims, pieces, -0.22, 0.18) if pieces else 1.0
    entries = jax.random.normal(own_key, dims, jnp.float32) * width * gain
    return jnp.minimum(jnp.maximum(entries, -most), most).astype(held_as)


def setup_inputs(seed: int = 0, part: int = 0) -> dict:
    splits = jax.random.split(jax.random.key(seed), 3)
    own_keys = jax.random.split(jax.random.fold_in(splits[2], part), 3)
    spectra = draw_spectra(jax.random.fold_in(jax.random.fold_in(splits[2], part), 71), part)
    probes = noise(own_keys[1], (PIXELS, K), 1.0, 6.0, ((0, 2),))
    return dict(spectra=spectra, probes=probes)


def reference(spectra, probes):
    loadings = lax.dot_general(spectra.astype(jnp.float32), probes.astype(jnp.float32), (((0,), (0,)), ((), ())), preferred_element_type=jnp.float32).astype(jnp.bfloat16)
    image = jnp.dot(spectra.astype(jnp.float32), loadings.astype(jnp.float32), preferred_element_type=jnp.float32)
    gram_matrix = lax.dot_general(image, image, (((0,), (0,)), ((), ())), precision=lax.Precision.HIGHEST) / jnp.float32(PIXELS)
    factor = jnp.linalg.cholesky(gram_matrix)
    basis = jax.scipy.linalg.solve_triangular(factor, image.T, lower=True).T
    return basis.reshape(N_PIX, PIX_DEV, K)
```

```python
import functools
import jax
import jax.numpy as jnp
from jax import lax
from jax.experimental import pallas as pl
from jax.experimental.pallas import tpu as pltpu
from jax.sharding import PartitionSpec as P

CHUNKS = 4
F32 = jnp.float32
BF16 = jnp.bfloat16
MIB = 1 << 20


def params(mib=32):
    return pltpu.CompilerParams(vmem_limit_bytes=mib * MIB)


def image_kernel(idx_ref, spectra_ref, loadings_ref, *out_refs):
    rows = out_refs[0].shape[1]
    for c, out in enumerate(out_refs):
        out[0] = jnp.dot(
            spectra_ref[0, 0, c * rows:(c + 1) * rows, :], loadings_ref[...], preferred_element_type=F32
        ).astype(out.dtype)


def image_half(idx, spectra, loadings, own, dtype):
    outer, _, rows, bins = spectra.shape
    cols = loadings.shape[1]
    piece = rows // CHUNKS
    side = (lambda i, idx: (i, idx[0], 0, 0)) if own else (lambda i, idx: (i, 1 - idx[0], 0, 0))
    return pl.pallas_call(
        image_kernel,
        grid_spec=pltpu.PrefetchScalarGridSpec(
            num_scalar_prefetch=1,
            grid=(outer,),
            in_specs=[
                pl.BlockSpec((1, 1, rows, bins), side),
                pl.BlockSpec((bins, cols), lambda i, idx: (0, 0)),
            ],
            out_specs=[pl.BlockSpec((1, piece, cols), lambda i, idx: (i, 0, 0))] * CHUNKS,
        ),
        out_shape=[jax.ShapeDtypeStruct((outer, piece, cols), dtype)] * CHUNKS,
        compiler_params=params(),
        cost_estimate=pl.CostEstimate(
            flops=2 * outer * rows * bins * cols, bytes_accessed=outer * rows * (bins * 2 + cols * 4), transcendentals=0
        ),
    )(idx, spectra, loadings)


def add_kernel(idx_ref, got_ref, kept_ref, own_ref, *send_refs):
    me = idx_ref[1]
    own_ref[...] = got_ref[me].astype(F32) + kept_ref[me]
    for d, send in enumerate(send_refs):
        other = lax.bitwise_xor(me, d + 1)
        send[...] = (got_ref[other].astype(F32) + kept_ref[other]).astype(send.dtype)


def add_chunk(idx, got, kept):
    outer, piece, cols = got.shape
    vmem = pl.BlockSpec(memory_space=pltpu.VMEM)
    return pl.pallas_call(
        add_kernel,
        in_specs=[pl.BlockSpec(memory_space=pltpu.SMEM), vmem, vmem],
        out_specs=[vmem] * outer,
        out_shape=[jax.ShapeDtypeStruct((piece, cols), F32)]
        + [jax.ShapeDtypeStruct((piece, cols), BF16)] * (outer - 1),
        compiler_params=params(),
        cost_estimate=pl.CostEstimate(
            flops=outer * piece * cols, bytes_accessed=outer * piece * cols * 8, transcendentals=0
        ),
    )(idx, got, kept)


def gram_kernel(n, *refs):
    own_ref, got, (gram_in, x_ref, gram_ref) = refs[0], refs[1:n], refs[n:]
    x = own_ref[...]
    for g in got:
        x = x + g[...].astype(F32)
    x_ref[...] = x
    gram_ref[...] = gram_in[...] + lax.dot_general(
        x, x, (((0,), (0,)), ((), ())), precision=lax.Precision.HIGHEST, preferred_element_type=F32
    )


def gram_chunk(own, got, gram):
    piece, cols = own.shape
    n = 1 + len(got)
    vmem = pl.BlockSpec(memory_space=pltpu.VMEM)
    return pl.pallas_call(
        functools.partial(gram_kernel, n),
        in_specs=[vmem] * (n + 1),
        out_specs=[vmem] * 2,
        out_shape=[jax.ShapeDtypeStruct((piece, cols), F32), jax.ShapeDtypeStruct((cols, cols), F32)],
        compiler_params=params(),
        cost_estimate=pl.CostEstimate(
            flops=12 * piece * cols * cols, bytes_accessed=n * piece * cols * 4, transcendentals=0
        ),
    )(own, *got, gram)


def xor_pairs(n, d):
    return [(i, i ^ d) for i in range(n)]


def on_device(n_bins, spectra, probes):
    rows_dev, bins = spectra.shape
    cols = probes.shape[1]
    outer = n_bins // 2
    rows = rows_dev // n_bins
    half = cols // 2
    me = lax.axis_index("bins")
    pix = lax.axis_index("pix")
    idx = jnp.stack([me % 2, me // 2]).astype(jnp.int32)

    terms = lax.dot_general(spectra, probes, (((0,), (0,)), ((), ())), preferred_element_type=F32)
    loadings = (terms + lax.ppermute(terms, "pix", xor_pairs(2, 1))).astype(BF16)

    blocks = spectra.reshape(outer, 2, rows, bins)
    away = image_half(idx, blocks, loadings, False, BF16)
    kept = image_half(idx, blocks, loadings, True, F32)
    gram = jnp.zeros((cols, cols), F32)
    image = []
    for c in range(CHUNKS):
        got = lax.ppermute(away[c], "bins", xor_pairs(n_bins, 1))
        own, *sends = add_chunk(idx, got, kept[c])
        arrived = [lax.ppermute(s, "bins", xor_pairs(n_bins, 2 * (d + 1))) for d, s in enumerate(sends)]
        x, gram = gram_chunk(own, arrived, gram)
        image.append(x)
    image_rows = jnp.concatenate(image, 0)

    corner = gram[half:, half:]
    lower = lax.broadcasted_iota(jnp.int32, (half, half), 0) >= lax.broadcasted_iota(jnp.int32, (half, half), 1)
    diag = jnp.sum(jnp.where(jnp.eye(half, dtype=bool), corner, 0.0), 0)
    packed = [
        jnp.concatenate([gram[half:, :half], jnp.zeros((8, half), F32)], 0),
        jnp.concatenate([jnp.where(lower, gram[:half, :half], corner), jnp.broadcast_to(diag, (8, half))], 0),
    ]
    mine = jnp.where(pix == 0, packed[0], packed[1])
    other = jnp.where(pix == 0, packed[1], packed[0])
    mine = mine + lax.ppermute(other, "pix", xor_pairs(2, 1))
    d = 1
    while d < n_bins:
        mine = mine + lax.ppermute(mine, "bins", xor_pairs(n_bins, d))
        d *= 2
    other = lax.ppermute(mine, "pix", xor_pairs(2, 1))
    below = jnp.where(pix == 0, mine, other)[:half]
    diags = jnp.where(pix == 0, other, mine)
    strict = jnp.where(lower, 0.0, diags[:half])
    first = jnp.where(lower, diags[:half], diags[:half].T)
    corner = strict + strict.T + jnp.where(jnp.eye(half, dtype=bool), diags[half], 0.0)
    gram_matrix = jnp.concatenate(
        [jnp.concatenate([first, below.T], 1), jnp.concatenate([below, corner], 1)], 0
    ) / F32(rows_dev * 2)

    factor = jnp.linalg.cholesky(gram_matrix)
    basis = jax.scipy.linalg.solve_triangular(factor, image_rows.T, lower=True).T
    return basis.reshape(1, rows, cols)


def solution(mesh):
    return jax.shard_map(
        functools.partial(on_device, mesh.shape["bins"]),
        mesh=mesh,
        in_specs=(P(("parts", "pix"), "bins"), P(("parts", "pix"), None)),
        out_specs=P(("parts", "pix"), "bins", None),
        check_vma=False,
    )
```

```python
import functools
import math
import jax
import jax.numpy as jnp
from jax import lax
from jax.experimental import pallas as pl
from jax.experimental.pallas import tpu as pltpu
from jax.sharding import PartitionSpec as P

CHUNKS = 4
PANEL = 16
F32 = jnp.float32
BF16 = jnp.bfloat16
MIB = 1 << 20


def params(mib=32):
    return pltpu.CompilerParams(vmem_limit_bytes=mib * MIB)


def image_kernel(idx_ref, spectra_ref, loadings_ref, *out_refs):
    rows = out_refs[0].shape[1]
    for c, out in enumerate(out_refs):
        out[0] = jnp.dot(
            spectra_ref[0, 0, c * rows:(c + 1) * rows, :], loadings_ref[...], preferred_element_type=F32
        ).astype(out.dtype)


def image_half(idx, spectra, loadings, own, dtype):
    outer, _, rows, bins = spectra.shape
    cols = loadings.shape[1]
    piece = rows // CHUNKS
    side = (lambda i, idx: (i, idx[0], 0, 0)) if own else (lambda i, idx: (i, 1 - idx[0], 0, 0))
    return pl.pallas_call(
        image_kernel,
        grid_spec=pltpu.PrefetchScalarGridSpec(
            num_scalar_prefetch=1,
            grid=(outer,),
            in_specs=[
                pl.BlockSpec((1, 1, rows, bins), side),
                pl.BlockSpec((bins, cols), lambda i, idx: (0, 0)),
            ],
            out_specs=[pl.BlockSpec((1, piece, cols), lambda i, idx: (i, 0, 0))] * CHUNKS,
        ),
        out_shape=[jax.ShapeDtypeStruct((outer, piece, cols), dtype)] * CHUNKS,
        compiler_params=params(),
        cost_estimate=pl.CostEstimate(
            flops=2 * outer * rows * bins * cols, bytes_accessed=outer * rows * (bins * 2 + cols * 4), transcendentals=0
        ),
    )(idx, spectra, loadings)


def add_kernel(idx_ref, got_ref, kept_ref, own_ref, *send_refs):
    me = idx_ref[1]
    own_ref[...] = got_ref[me].astype(F32) + kept_ref[me]
    for d, send in enumerate(send_refs):
        other = lax.bitwise_xor(me, d + 1)
        send[...] = (got_ref[other].astype(F32) + kept_ref[other]).astype(send.dtype)


def add_chunk(idx, got, kept):
    outer, piece, cols = got.shape
    vmem = pl.BlockSpec(memory_space=pltpu.VMEM)
    return pl.pallas_call(
        add_kernel,
        in_specs=[pl.BlockSpec(memory_space=pltpu.SMEM), vmem, vmem],
        out_specs=[vmem] * outer,
        out_shape=[jax.ShapeDtypeStruct((piece, cols), F32)]
        + [jax.ShapeDtypeStruct((piece, cols), BF16)] * (outer - 1),
        compiler_params=params(),
        cost_estimate=pl.CostEstimate(
            flops=outer * piece * cols, bytes_accessed=outer * piece * cols * 8, transcendentals=0
        ),
    )(idx, got, kept)


def gram_kernel(n, last, *refs):
    if last:
        pix_ref, refs = refs[0], refs[1:]
    own_ref, got, (gram_in, x_ref, *out) = refs[0], refs[1:n], refs[n:]
    x = own_ref[...]
    for g in got:
        x = x + g[...].astype(F32)
    x_ref[...] = x
    gram = gram_in[...] + lax.dot_general(
        x, x, (((0,), (0,)), ((), ())), precision=lax.Precision.HIGHEST, preferred_element_type=F32
    )
    if not last:
        out[0][...] = gram
        return
    half = gram.shape[0] // 2
    mine, other = out
    row = lax.broadcasted_iota(jnp.int32, (half, half), 0)
    col = lax.broadcasted_iota(jnp.int32, (half, half), 1)
    corner = gram[half:, half:]
    diag = jnp.sum(jnp.where(row == col, corner, 0.0), 0, keepdims=True)
    above = gram[:half, half:]
    both = jnp.where(row >= col, gram[:half, :half], corner)
    first = pix_ref[0] == 0
    mine[:half] = jnp.where(first, above, both)
    other[:half] = jnp.where(first, both, above)
    mine[half:] = jnp.broadcast_to(diag, (8, half))
    other[half:] = jnp.broadcast_to(diag, (8, half))


def gram_chunk(own, got, gram, pix=None):
    piece, cols = own.shape
    n = 1 + len(got)
    half = cols // 2
    vmem = pl.BlockSpec(memory_space=pltpu.VMEM)
    last = pix is not None
    shapes = [(half + 8, half)] * 2 if last else [(cols, cols)]
    return pl.pallas_call(
        functools.partial(gram_kernel, n, last),
        in_specs=[pl.BlockSpec(memory_space=pltpu.SMEM)] * last + [vmem] * (n + 1),
        out_specs=[vmem] * (1 + len(shapes)),
        out_shape=[jax.ShapeDtypeStruct(s, F32) for s in [(piece, cols)] + shapes],
        compiler_params=params(),
        cost_estimate=pl.CostEstimate(
            flops=12 * piece * cols * cols, bytes_accessed=n * piece * cols * 4, transcendentals=0
        ),
    )(*[pix] * last, own, *got, gram)


def transposed_dot(a, b):
    return lax.dot_general(
        a, b, (((0,), (0,)), ((), ())), precision=lax.Precision.HIGHEST, preferred_element_type=F32
    )


def wide(column, width):
    return column if width == 128 else jnp.concatenate([column] * (width // 128), 1)


def invert_factor(gram, inverse):
    n = gram.shape[0]
    row = lax.broadcasted_iota(jnp.int32, (PANEL, 128), 0)
    for k in range(0, n, PANEL):
        end = k + PANEL
        start, reach = k // 128 * 128, -(-end // 128) * 128
        right, left = gram[k:end, start:n], inverse[k:end, :reach]
        width = n - start
        columns = [jnp.broadcast_to(right[:, k - start + j:k - start + j + 1], (PANEL, 128)) for j in range(PANEL)]
        pivots = jnp.ones((PANEL, 128), F32)
        for j in range(0, PANEL, 2):
            c0, c1 = columns[j], columns[j + 1]
            a, b, c = c0[j:j + 1], c1[j:j + 1], c1[j + 1:j + 2]
            det = a * c - b * b
            inv_a, inv_det = 1.0 / a, 1.0 / det
            pivots = jnp.where(row == j, a, jnp.where(row == j + 1, det * inv_a, pivots))
            below = row > j + 1
            g0 = jnp.where(below, (c0 * c - c1 * b) * inv_det, jnp.where(row == j + 1, b * inv_a, 0.0))
            g1 = jnp.where(below, (c1 * a - c0 * b) * inv_det, 0.0)
            for m in range(j + 2, PANEL):
                columns[m] = columns[m] - g0 * columns[m][j:j + 1] - g1 * columns[m][j + 1:j + 2]
            right = right - wide(g0, width) * right[j:j + 1] - wide(g1, width) * right[j + 1:j + 2]
            left = left - wide(g0, reach) * left[j:j + 1] - wide(g1, reach) * left[j + 1:j + 2]
        scale = lax.rsqrt(pivots)
        right, left = right * wide(scale, width), left * wide(scale, reach)
        inverse[k:end, :reach] = left
        if end < n:
            base = end // 128 * 128
            rest = right[:, base - start:]
            gram[end:n, base:n] = gram[end:n, base:n] - transposed_dot(rest, rest)[end - base:]
            inverse[end:n, :reach] = inverse[end:n, :reach] - transposed_dot(rest, left)[end - base:]


def basis_kernel(pixels, pix_ref, mine_ref, other_ref, *refs):
    pieces, (basis_ref, gram, inverse) = refs[:-3], refs[-3:]
    n = gram.shape[0]
    half = n // 2
    first = pix_ref[0] == 0
    mine, other = mine_ref[...], other_ref[...]
    above = jnp.where(first, mine[:half], other[:half])
    both = jnp.where(first, other, mine)
    row = lax.broadcasted_iota(jnp.int32, (half, half), 0)
    col = lax.broadcasted_iota(jnp.int32, (half, half), 1)
    eye = row == col
    both, corner = both[:half], both[half:half + 1]
    turned = both.T
    blocks = [jnp.where(row >= col, both, turned), jnp.where(eye, corner, jnp.where(row > col, turned, both))]
    across = [lax.rsqrt(jnp.sum(jnp.where(eye, blk, 0.0), 0, keepdims=True)) for blk in blocks]
    down = [lax.rsqrt(jnp.sum(jnp.where(eye, blk, 0.0), 1, keepdims=True)) for blk in blocks]
    gram[:half, :half] = blocks[0] * across[0] * down[0]
    gram[:half, half:] = above * across[1] * down[0]
    gram[half:, half:] = blocks[1] * across[1] * down[1]
    zero = jnp.zeros((half, half), F32)
    root = math.sqrt(pixels)
    inverse[:half, :half] = jnp.where(eye, jnp.broadcast_to(across[0] * root, (half, half)), 0.0)
    inverse[half:, half:] = jnp.where(eye, jnp.broadcast_to(across[1] * root, (half, half)), 0.0)
    inverse[:half, half:] = zero
    inverse[half:, :half] = zero
    invert_factor(gram, inverse)
    rows = 0
    for x in pieces:
        basis_ref[rows:rows + x.shape[0]] = lax.dot_general(
            x[...], inverse[...], (((1,), (1,)), ((), ())),
            precision=lax.Precision.HIGHEST, preferred_element_type=F32,
        )
        rows += x.shape[0]


def basis_of(pix, mine, other, image, pixels):
    cols = image[0].shape[1]
    rows = sum(x.shape[0] for x in image)
    vmem = pl.BlockSpec(memory_space=pltpu.VMEM)
    return pl.pallas_call(
        functools.partial(basis_kernel, pixels),
        in_specs=[pl.BlockSpec(memory_space=pltpu.SMEM)] + [vmem] * (2 + len(image)),
        out_specs=vmem,
        out_shape=jax.ShapeDtypeStruct((rows, cols), F32),
        scratch_shapes=[pltpu.VMEM((cols, cols), F32)] * 2,
        compiler_params=params(),
    )(pix, mine, other, *image)


def xor_pairs(n, d):
    return [(i, i ^ d) for i in range(n)]


def on_device(n_bins, spectra, probes):
    rows_dev, bins = spectra.shape
    cols = probes.shape[1]
    outer = n_bins // 2
    rows = rows_dev // n_bins
    me = lax.axis_index("bins")
    pix = lax.axis_index("pix").astype(jnp.int32).reshape(1)
    idx = jnp.stack([me % 2, me // 2]).astype(jnp.int32)

    terms = lax.dot_general(spectra, probes, (((0,), (0,)), ((), ())), preferred_element_type=F32)
    loadings = (terms + lax.ppermute(terms, "pix", xor_pairs(2, 1))).astype(BF16)

    blocks = spectra.reshape(outer, 2, rows, bins)
    away = image_half(idx, blocks, loadings, False, BF16)
    kept = image_half(idx, blocks, loadings, True, F32)
    gram = jnp.zeros((cols, cols), F32)
    image = []
    for c in range(CHUNKS):
        got = lax.ppermute(away[c], "bins", xor_pairs(n_bins, 1))
        own, *sends = add_chunk(idx, got, kept[c])
        arrived = [lax.ppermute(s, "bins", xor_pairs(n_bins, 2 * (d + 1))) for d, s in enumerate(sends)]
        if c < CHUNKS - 1:
            x, gram = gram_chunk(own, arrived, gram)
        else:
            x, mine, other = gram_chunk(own, arrived, gram, pix)
        image.append(x)

    mine = mine + lax.ppermute(other, "pix", xor_pairs(2, 1))
    d = 1
    while d < n_bins:
        mine = mine + lax.ppermute(mine, "bins", xor_pairs(n_bins, d))
        d *= 2
    other = lax.ppermute(mine, "pix", xor_pairs(2, 1))
    basis = basis_of(pix, mine, other, image, 2 * rows_dev)
    return basis.reshape(1, rows, cols)


def solution(mesh):
    return jax.shard_map(
        functools.partial(on_device, mesh.shape["bins"]),
        mesh=mesh,
        in_specs=(P(("parts", "pix"), "bins"), P(("parts", "pix"), None)),
        out_specs=P(("parts", "pix"), "bins", None),
        check_vma=False,
    )
```

```python
import functools
import math
import jax
import jax.numpy as jnp
from jax import lax
from jax.experimental import pallas as pl
from jax.experimental.pallas import tpu as pltpu
from jax.sharding import PartitionSpec as P

SHARES = (1, 1, 1)
PIECES = 8
PANEL = 16
F32 = jnp.float32
BF16 = jnp.bfloat16
MIB = 1 << 20
VMEM = pl.BlockSpec(memory_space=pltpu.VMEM)
SMEM = pl.BlockSpec(memory_space=pltpu.SMEM)
HBM = pl.BlockSpec(memory_space=pltpu.HBM)


def params(mib=32):
    return pltpu.CompilerParams(vmem_limit_bytes=mib * MIB)


def loadings_kernel(spectra_hbm, probes_hbm, terms_ref, spectra_ref, probes_ref, sems):
    rows = spectra_ref.shape[0] // PIECES

    def copies(i):
        part = pl.ds(i * rows, rows)
        return (
            pltpu.make_async_copy(probes_hbm.at[part], probes_ref.at[part], sems.at[0, i]),
            pltpu.make_async_copy(spectra_hbm.at[part], spectra_ref.at[part], sems.at[1, i]),
        )

    for i in range(PIECES):
        for copy in copies(i):
            copy.start()
    for i in range(PIECES):
        for copy in copies(i):
            copy.wait()
        part = pl.ds(i * rows, rows)
        term = lax.dot_general(
            probes_ref[part], spectra_ref[part], (((0,), (0,)), ((), ())), preferred_element_type=F32
        )
        if i == 0:
            terms_ref[...] = term
        else:
            terms_ref[...] += term


def loadings_terms(spectra, probes):
    rows, bins = spectra.shape
    cols = probes.shape[1]
    return pl.pallas_call(
        loadings_kernel,
        in_specs=[HBM, HBM],
        out_specs=VMEM,
        out_shape=jax.ShapeDtypeStruct((cols, bins), F32),
        scratch_shapes=[
            pltpu.VMEM((rows, bins), BF16),
            pltpu.VMEM((rows, cols), BF16),
            pltpu.SemaphoreType.DMA((2, PIECES)),
        ],
        compiler_params=params(51),
        cost_estimate=pl.CostEstimate(
            flops=2 * rows * bins * cols, bytes_accessed=rows * (bins + cols) * 2, transcendentals=0
        ),
    )(spectra, probes)


def block_copies(spectra_hbm, blocks_ref, sems, side):
    outer, rows, _ = blocks_ref.shape
    starts = [pl.multiple_of((i * 2 + side) * rows, 16) for i in range(outer)]
    return [
        pltpu.make_async_copy(spectra_hbm.at[pl.ds(start, rows)], blocks_ref.at[i], sems.at[i])
        for i, start in enumerate(starts)
    ]


def fetch_kernel(idx_ref, spectra_hbm, after_ref, blocks_ref, sems):
    copies = block_copies(spectra_hbm, blocks_ref, sems, 1 - idx_ref[0])
    for copy in copies:
        copy.start()
    for copy in copies:
        copy.wait()


def fetch_blocks(idx, spectra, rows, after):
    outer, bins = spectra.shape[0] // (2 * rows), spectra.shape[1]
    return pl.pallas_call(
        fetch_kernel,
        in_specs=[SMEM, HBM, pl.BlockSpec(memory_space=pl.ANY)],
        out_specs=VMEM,
        out_shape=jax.ShapeDtypeStruct((outer, rows, bins), BF16),
        scratch_shapes=[pltpu.SemaphoreType.DMA((outer,))],
        compiler_params=params(48),
        cost_estimate=pl.CostEstimate(flops=0, bytes_accessed=outer * rows * bins * 4, transcendentals=0),
    )(idx, spectra, after)


def away_kernel(blocks_ref, mine_ref, got_ref, loadings_ref, *out_refs):
    loadings_ref[...] = (mine_ref[...] + got_ref[...]).T.astype(BF16)
    first = 0
    for out_ref in out_refs:
        size = out_ref.shape[1]
        for i in range(out_ref.shape[0]):
            out_ref[i] = jnp.dot(
                blocks_ref[i, first:first + size], loadings_ref[...], preferred_element_type=F32
            ).astype(out_ref.dtype)
        first += size


def image_away(blocks, mine, got, sizes):
    outer, rows, bins = blocks.shape
    cols = mine.shape[0]
    shapes = [jax.ShapeDtypeStruct((bins, cols), BF16)]
    shapes += [jax.ShapeDtypeStruct((outer, size, cols), BF16) for size in sizes]
    return pl.pallas_call(
        away_kernel,
        in_specs=[VMEM] * 3,
        out_specs=[VMEM] * len(shapes),
        out_shape=shapes,
        compiler_params=params(),
        cost_estimate=pl.CostEstimate(
            flops=2 * outer * rows * bins * cols, bytes_accessed=outer * rows * cols * 4, transcendentals=0
        ),
    )(blocks, mine, got)


def kept_kernel(idx_ref, spectra_hbm, loadings_ref, *refs):
    *out_refs, blocks_ref, sems = refs
    copies = block_copies(spectra_hbm, blocks_ref, sems, idx_ref[0])
    for copy in copies:
        copy.start()
    for i, copy in enumerate(copies):
        copy.wait()
        first = 0
        for out_ref in out_refs:
            size = out_ref.shape[1]
            out_ref[i] = jnp.dot(
                blocks_ref[i, first:first + size], loadings_ref[...], preferred_element_type=F32
            )
            first += size


def image_kept(idx, spectra, loadings, sizes):
    rows = sum(sizes)
    outer, (bins, cols) = spectra.shape[0] // (2 * rows), loadings.shape
    return pl.pallas_call(
        kept_kernel,
        in_specs=[SMEM, HBM, VMEM],
        out_specs=[VMEM] * len(sizes),
        out_shape=[jax.ShapeDtypeStruct((outer, size, cols), F32) for size in sizes],
        scratch_shapes=[pltpu.VMEM((outer, rows, bins), BF16), pltpu.SemaphoreType.DMA((outer,))],
        compiler_params=params(48),
        cost_estimate=pl.CostEstimate(
            flops=2 * outer * rows * bins * cols, bytes_accessed=outer * rows * (bins * 2 + cols * 4), transcendentals=0
        ),
    )(idx, spectra, loadings)


def add_kernel(n_after, idx_ref, got_ref, kept_ref, *refs):
    own_ref, *send_refs = refs[n_after:]
    me = idx_ref[1]
    own_ref[...] = got_ref[me].astype(F32) + kept_ref[me]
    for d, send in enumerate(send_refs):
        other = lax.bitwise_xor(me, d + 1)
        send[...] = (got_ref[other].astype(F32) + kept_ref[other]).astype(send.dtype)


def add_chunk(idx, got, kept, after):
    outer, piece, cols = got.shape
    return pl.pallas_call(
        functools.partial(add_kernel, len(after)),
        in_specs=[SMEM, VMEM, VMEM] + [pl.BlockSpec(memory_space=pl.ANY)] * len(after),
        out_specs=[VMEM] * outer,
        out_shape=[jax.ShapeDtypeStruct((piece, cols), F32)]
        + [jax.ShapeDtypeStruct((piece, cols), BF16)] * (outer - 1),
        compiler_params=params(),
        cost_estimate=pl.CostEstimate(
            flops=outer * piece * cols, bytes_accessed=outer * piece * cols * 8, transcendentals=0
        ),
    )(idx, got, kept, *after)


def gram_kernel(n, last, *refs):
    if last:
        pix_ref, refs = refs[0], refs[1:]
    own_ref, got, (gram_in, x_ref, *out) = refs[0], refs[1:n], refs[n:]
    x = own_ref[...]
    for g in got:
        x = x + g[...].astype(F32)
    x_ref[...] = x
    gram = gram_in[...] + lax.dot_general(
        x, x, (((0,), (0,)), ((), ())), precision=lax.Precision.HIGHEST, preferred_element_type=F32
    )
    if not last:
        out[0][...] = gram
        return
    half = gram.shape[0] // 2
    mine, other = out
    row = lax.broadcasted_iota(jnp.int32, (half, half), 0)
    col = lax.broadcasted_iota(jnp.int32, (half, half), 1)
    corner = gram[half:, half:]
    diag = jnp.sum(jnp.where(row == col, corner, 0.0), 0, keepdims=True)
    above = gram[:half, half:]
    both = jnp.where(row >= col, gram[:half, :half], corner)
    first = pix_ref[0] == 0
    mine[:half] = jnp.where(first, above, both)
    other[:half] = jnp.where(first, both, above)
    mine[half:] = jnp.broadcast_to(diag, (8, half))
    other[half:] = jnp.broadcast_to(diag, (8, half))


def gram_chunk(own, got, gram, pix=None):
    piece, cols = own.shape
    n = 1 + len(got)
    half = cols // 2
    last = pix is not None
    shapes = [(half + 8, half)] * 2 if last else [(cols, cols)]
    return pl.pallas_call(
        functools.partial(gram_kernel, n, last),
        in_specs=[SMEM] * last + [VMEM] * (n + 1),
        out_specs=[VMEM] * (1 + len(shapes)),
        out_shape=[jax.ShapeDtypeStruct(s, F32) for s in [(piece, cols)] + shapes],
        compiler_params=params(),
        cost_estimate=pl.CostEstimate(
            flops=12 * piece * cols * cols, bytes_accessed=n * piece * cols * 4, transcendentals=0
        ),
    )(*[pix] * last, own, *got, gram)


def transposed_dot(a, b):
    return lax.dot_general(
        a, b, (((0,), (0,)), ((), ())), precision=lax.Precision.HIGHEST, preferred_element_type=F32
    )


def wide(column, width):
    return column if width == 128 else jnp.concatenate([column] * (width // 128), 1)


def invert_factor(gram, inverse):
    n = gram.shape[0]
    row = lax.broadcasted_iota(jnp.int32, (PANEL, 128), 0)
    for k in range(0, n, PANEL):
        end = k + PANEL
        start, reach = k // 128 * 128, -(-end // 128) * 128
        right, left = gram[k:end, start:n], inverse[k:end, :reach]
        width = n - start
        columns = [jnp.broadcast_to(right[:, k - start + j:k - start + j + 1], (PANEL, 128)) for j in range(PANEL)]
        pivots = jnp.ones((PANEL, 128), F32)
        for j in range(0, PANEL, 2):
            c0, c1 = columns[j], columns[j + 1]
            a, b, c = c0[j:j + 1], c1[j:j + 1], c1[j + 1:j + 2]
            det = a * c - b * b
            inv_a, inv_det = 1.0 / a, 1.0 / det
            pivots = jnp.where(row == j, a, jnp.where(row == j + 1, det * inv_a, pivots))
            below = row > j + 1
            g0 = jnp.where(below, (c0 * c - c1 * b) * inv_det, jnp.where(row == j + 1, b * inv_a, 0.0))
            g1 = jnp.where(below, (c1 * a - c0 * b) * inv_det, 0.0)
            for m in range(j + 2, PANEL):
                columns[m] = columns[m] - g0 * columns[m][j:j + 1] - g1 * columns[m][j + 1:j + 2]
            right = right - wide(g0, width) * right[j:j + 1] - wide(g1, width) * right[j + 1:j + 2]
            left = left - wide(g0, reach) * left[j:j + 1] - wide(g1, reach) * left[j + 1:j + 2]
        scale = lax.rsqrt(pivots)
        right, left = right * wide(scale, width), left * wide(scale, reach)
        inverse[k:end, :reach] = left
        if end < n:
            base = end // 128 * 128
            rest = right[:, base - start:]
            gram[end:n, base:n] = gram[end:n, base:n] - transposed_dot(rest, rest)[end - base:]
            inverse[end:n, :reach] = inverse[end:n, :reach] - transposed_dot(rest, left)[end - base:]


def basis_kernel(pixels, pix_ref, mine_ref, other_ref, *refs):
    pieces, (basis_ref, gram, inverse) = refs[:-3], refs[-3:]
    n = gram.shape[0]
    half = n // 2
    first = pix_ref[0] == 0
    mine, other = mine_ref[...], other_ref[...]
    above = jnp.where(first, mine[:half], other[:half])
    both = jnp.where(first, other, mine)
    row = lax.broadcasted_iota(jnp.int32, (half, half), 0)
    col = lax.broadcasted_iota(jnp.int32, (half, half), 1)
    eye = row == col
    both, corner = both[:half], both[half:half + 1]
    turned = both.T
    blocks = [jnp.where(row >= col, both, turned), jnp.where(eye, corner, jnp.where(row > col, turned, both))]
    across = [lax.rsqrt(jnp.sum(jnp.where(eye, blk, 0.0), 0, keepdims=True)) for blk in blocks]
    down = [lax.rsqrt(jnp.sum(jnp.where(eye, blk, 0.0), 1, keepdims=True)) for blk in blocks]
    gram[:half, :half] = blocks[0] * across[0] * down[0]
    gram[:half, half:] = above * across[1] * down[0]
    gram[half:, half:] = blocks[1] * across[1] * down[1]
    zero = jnp.zeros((half, half), F32)
    root = math.sqrt(pixels)
    inverse[:half, :half] = jnp.where(eye, jnp.broadcast_to(across[0] * root, (half, half)), 0.0)
    inverse[half:, half:] = jnp.where(eye, jnp.broadcast_to(across[1] * root, (half, half)), 0.0)
    inverse[:half, half:] = zero
    inverse[half:, :half] = zero
    invert_factor(gram, inverse)
    rows = 0
    for x in pieces:
        basis_ref[rows:rows + x.shape[0]] = lax.dot_general(
            x[...], inverse[...], (((1,), (1,)), ((), ())),
            precision=lax.Precision.HIGHEST, preferred_element_type=F32,
        )
        rows += x.shape[0]


def basis_of(pix, mine, other, image, pixels):
    cols = image[0].shape[1]
    rows = sum(x.shape[0] for x in image)
    return pl.pallas_call(
        functools.partial(basis_kernel, pixels),
        in_specs=[SMEM] + [VMEM] * (2 + len(image)),
        out_specs=VMEM,
        out_shape=jax.ShapeDtypeStruct((rows, cols), F32),
        scratch_shapes=[pltpu.VMEM((cols, cols), F32)] * 2,
        compiler_params=params(),
    )(pix, mine, other, *image)


def split(rows):
    ends = [-(-rows // 16 * sum(SHARES[:k]) // sum(SHARES)) * 16 for k in range(len(SHARES) + 1)]
    return [last - first for first, last in zip(ends, ends[1:]) if last > first]


def xor_pairs(n, d):
    return [(i, i ^ d) for i in range(n)]


def on_device(n_bins, spectra, probes):
    rows_dev, bins = spectra.shape
    cols = probes.shape[1]
    rows = rows_dev // n_bins
    me = lax.axis_index("bins")
    pix = lax.axis_index("pix").astype(jnp.int32).reshape(1)
    idx = jnp.stack([me % 2, me // 2]).astype(jnp.int32)

    sizes = split(rows)
    terms = loadings_terms(spectra, probes)
    got = lax.ppermute(terms, "pix", xor_pairs(2, 1))
    blocks = fetch_blocks(idx, spectra, rows, terms)
    loadings, *away = image_away(blocks, terms, got, sizes)
    away = [lax.ppermute(out, "bins", xor_pairs(n_bins, 1)) for out in away]
    kept = image_kept(idx, spectra, loadings, sizes)
    gram = jnp.zeros((cols, cols), F32)
    image = []
    for c in range(len(sizes)):
        own, *sends = add_chunk(idx, away[c], kept[c], image[c - 2:c - 1] if c > 1 else [])
        arrived = [lax.ppermute(s, "bins", xor_pairs(n_bins, 2 * (d + 1))) for d, s in enumerate(sends)]
        if c < len(sizes) - 1:
            x, gram = gram_chunk(own, arrived, gram)
        else:
            x, mine, other = gram_chunk(own, arrived, gram, pix)
        image.append(x)

    mine = mine + lax.ppermute(other, "pix", xor_pairs(2, 1))
    d = 1
    while d < n_bins:
        mine = mine + lax.ppermute(mine, "bins", xor_pairs(n_bins, d))
        d *= 2
    other = lax.ppermute(mine, "pix", xor_pairs(2, 1))
    basis = basis_of(pix, mine, other, image, 2 * rows_dev)
    return basis.reshape(1, rows, cols)


def solution(mesh):
    return jax.shard_map(
        functools.partial(on_device, mesh.shape["bins"]),
        mesh=mesh,
        in_specs=(P(("parts", "pix"), "bins"), P(("parts", "pix"), None)),
        out_specs=P(("parts", "pix"), "bins", None),
        check_vma=False,
    )
```

```python
import functools
import math
import jax
import jax.numpy as jnp
from jax import lax
from jax.experimental import pallas as pl
from jax.experimental.pallas import tpu as pltpu
from jax.sharding import PartitionSpec as P

SHARES = (1, 1, 1)
PIECES = 8
PANEL = 16
WINDOW = 32
F32 = jnp.float32
BF16 = jnp.bfloat16
MIB = 1 << 20
VMEM = pl.BlockSpec(memory_space=pltpu.VMEM)
SMEM = pl.BlockSpec(memory_space=pltpu.SMEM)
HBM = pl.BlockSpec(memory_space=pltpu.HBM)


def params(mib=32):
    return pltpu.CompilerParams(vmem_limit_bytes=mib * MIB)


def loadings_kernel(spectra_hbm, probes_hbm, terms_ref, spectra_ref, probes_ref, sems):
    rows = spectra_ref.shape[0] // PIECES

    def copies(i):
        part = pl.ds(i * rows, rows)
        return (
            pltpu.make_async_copy(probes_hbm.at[part], probes_ref.at[part], sems.at[0, i]),
            pltpu.make_async_copy(spectra_hbm.at[part], spectra_ref.at[part], sems.at[1, i]),
        )

    for i in range(PIECES):
        for copy in copies(i):
            copy.start()
    for i in range(PIECES):
        for copy in copies(i):
            copy.wait()
        part = pl.ds(i * rows, rows)
        term = lax.dot_general(
            probes_ref[part], spectra_ref[part], (((0,), (0,)), ((), ())), preferred_element_type=F32
        )
        if i == 0:
            terms_ref[...] = term
        else:
            terms_ref[...] += term


def loadings_terms(spectra, probes):
    rows, bins = spectra.shape
    cols = probes.shape[1]
    return pl.pallas_call(
        loadings_kernel,
        in_specs=[HBM, HBM],
        out_specs=VMEM,
        out_shape=jax.ShapeDtypeStruct((cols, bins), F32),
        scratch_shapes=[
            pltpu.VMEM((rows, bins), BF16),
            pltpu.VMEM((rows, cols), BF16),
            pltpu.SemaphoreType.DMA((2, PIECES)),
        ],
        compiler_params=params(51),
        cost_estimate=pl.CostEstimate(
            flops=2 * rows * bins * cols, bytes_accessed=rows * (bins + cols) * 2, transcendentals=0
        ),
    )(spectra, probes)


def block_copies(spectra_hbm, blocks_ref, sems, side):
    outer, rows, _ = blocks_ref.shape
    starts = [pl.multiple_of((i * 2 + side) * rows, 16) for i in range(outer)]
    return [
        pltpu.make_async_copy(spectra_hbm.at[pl.ds(start, rows)], blocks_ref.at[i], sems.at[i])
        for i, start in enumerate(starts)
    ]


def fetch_kernel(idx_ref, spectra_hbm, after_ref, blocks_ref, sems):
    copies = block_copies(spectra_hbm, blocks_ref, sems, 1 - idx_ref[0])
    for copy in copies:
        copy.start()
    for copy in copies:
        copy.wait()


def fetch_blocks(idx, spectra, rows, after):
    outer, bins = spectra.shape[0] // (2 * rows), spectra.shape[1]
    return pl.pallas_call(
        fetch_kernel,
        in_specs=[SMEM, HBM, pl.BlockSpec(memory_space=pl.ANY)],
        out_specs=VMEM,
        out_shape=jax.ShapeDtypeStruct((outer, rows, bins), BF16),
        scratch_shapes=[pltpu.SemaphoreType.DMA((outer,))],
        compiler_params=params(48),
        cost_estimate=pl.CostEstimate(flops=0, bytes_accessed=outer * rows * bins * 4, transcendentals=0),
    )(idx, spectra, after)


def away_kernel(blocks_ref, mine_ref, got_ref, loadings_ref, *out_refs):
    loadings_ref[...] = (mine_ref[...] + got_ref[...]).T.astype(BF16)
    first = 0
    for out_ref in out_refs:
        size = out_ref.shape[1]
        for i in range(out_ref.shape[0]):
            out_ref[i] = jnp.dot(
                blocks_ref[i, first:first + size], loadings_ref[...], preferred_element_type=F32
            ).astype(out_ref.dtype)
        first += size


def image_away(blocks, mine, got, sizes):
    outer, rows, bins = blocks.shape
    cols = mine.shape[0]
    shapes = [jax.ShapeDtypeStruct((bins, cols), BF16)]
    shapes += [jax.ShapeDtypeStruct((outer, size, cols), BF16) for size in sizes]
    return pl.pallas_call(
        away_kernel,
        in_specs=[VMEM] * 3,
        out_specs=[VMEM] * len(shapes),
        out_shape=shapes,
        compiler_params=params(),
        cost_estimate=pl.CostEstimate(
            flops=2 * outer * rows * bins * cols, bytes_accessed=outer * rows * cols * 4, transcendentals=0
        ),
    )(blocks, mine, got)


def kept_kernel(idx_ref, spectra_hbm, loadings_ref, *refs):
    *out_refs, blocks_ref, sems = refs
    copies = block_copies(spectra_hbm, blocks_ref, sems, idx_ref[0])
    for copy in copies:
        copy.start()
    for i, copy in enumerate(copies):
        copy.wait()
        first = 0
        for out_ref in out_refs:
            size = out_ref.shape[1]
            out_ref[i] = jnp.dot(
                blocks_ref[i, first:first + size], loadings_ref[...], preferred_element_type=F32
            )
            first += size


def image_kept(idx, spectra, loadings, sizes):
    rows = sum(sizes)
    outer, (bins, cols) = spectra.shape[0] // (2 * rows), loadings.shape
    return pl.pallas_call(
        kept_kernel,
        in_specs=[SMEM, HBM, VMEM],
        out_specs=[VMEM] * len(sizes),
        out_shape=[jax.ShapeDtypeStruct((outer, size, cols), F32) for size in sizes],
        scratch_shapes=[pltpu.VMEM((outer, rows, bins), BF16), pltpu.SemaphoreType.DMA((outer,))],
        compiler_params=params(48),
        cost_estimate=pl.CostEstimate(
            flops=2 * outer * rows * bins * cols, bytes_accessed=outer * rows * (bins * 2 + cols * 4), transcendentals=0
        ),
    )(idx, spectra, loadings)


def add_kernel(n_after, idx_ref, got_ref, kept_ref, *refs):
    own_ref, *send_refs = refs[n_after:]
    me = idx_ref[1]
    own_ref[...] = got_ref[me].astype(F32) + kept_ref[me]
    for d, send in enumerate(send_refs):
        other = lax.bitwise_xor(me, d + 1)
        send[...] = (got_ref[other].astype(F32) + kept_ref[other]).astype(send.dtype)


def add_chunk(idx, got, kept, after):
    outer, piece, cols = got.shape
    return pl.pallas_call(
        functools.partial(add_kernel, len(after)),
        in_specs=[SMEM, VMEM, VMEM] + [pl.BlockSpec(memory_space=pl.ANY)] * len(after),
        out_specs=[VMEM] * outer,
        out_shape=[jax.ShapeDtypeStruct((piece, cols), F32)]
        + [jax.ShapeDtypeStruct((piece, cols), BF16)] * (outer - 1),
        compiler_params=params(),
        cost_estimate=pl.CostEstimate(
            flops=outer * piece * cols, bytes_accessed=outer * piece * cols * 8, transcendentals=0
        ),
    )(idx, got, kept, *after)


def gram_kernel(n, last, *refs):
    if last:
        pix_ref, refs = refs[0], refs[1:]
    own_ref, got, (gram_in, x_ref, *out) = refs[0], refs[1:n], refs[n:]
    x = own_ref[...]
    for g in got:
        x = x + g[...].astype(F32)
    x_ref[...] = x
    gram = gram_in[...] + lax.dot_general(
        x, x, (((0,), (0,)), ((), ())), precision=lax.Precision.HIGHEST, preferred_element_type=F32
    )
    if not last:
        out[0][...] = gram
        return
    half = gram.shape[0] // 2
    mine, other = out
    row = lax.broadcasted_iota(jnp.int32, (half, half), 0)
    col = lax.broadcasted_iota(jnp.int32, (half, half), 1)
    corner = gram[half:, half:]
    diag = jnp.sum(jnp.where(row == col, corner, 0.0), 0, keepdims=True)
    above = gram[:half, half:]
    both = jnp.where(row >= col, gram[:half, :half], corner)
    first = pix_ref[0] == 0
    mine[:half] = jnp.where(first, above, both)
    other[:half] = jnp.where(first, both, above)
    mine[half:] = jnp.broadcast_to(diag, (8, half))
    other[half:] = jnp.broadcast_to(diag, (8, half))


def gram_chunk(own, got, gram, pix=None):
    piece, cols = own.shape
    n = 1 + len(got)
    half = cols // 2
    last = pix is not None
    shapes = [(half + 8, half)] * 2 if last else [(cols, cols)]
    return pl.pallas_call(
        functools.partial(gram_kernel, n, last),
        in_specs=[SMEM] * last + [VMEM] * (n + 1),
        out_specs=[VMEM] * (1 + len(shapes)),
        out_shape=[jax.ShapeDtypeStruct(s, F32) for s in [(piece, cols)] + shapes],
        compiler_params=params(),
        cost_estimate=pl.CostEstimate(
            flops=12 * piece * cols * cols, bytes_accessed=n * piece * cols * 4, transcendentals=0
        ),
    )(*[pix] * last, own, *got, gram)


def transposed_dot(a, b):
    def terms(x):
        high = x.astype(BF16)
        rest = x - high.astype(F32)
        middle = rest.astype(BF16)
        return high, middle, (rest - middle.astype(F32)).astype(BF16)

    (a0, a1, a2), (b0, b1, b2) = terms(a), terms(b)
    return lax.dot_general(
        jnp.concatenate([a0, a0, a1, a1, a0, a2], 0), jnp.concatenate([b0, b1, b0, b1, b2, b0], 0),
        (((0,), (0,)), ((), ())), preferred_element_type=F32,
    )


def wide(column, width):
    return column if width == 128 else jnp.concatenate([column] * (width // 128), 1)


def eliminate_panel(right, left, at):
    rows, width = right.shape
    reach = left.shape[1]
    row = lax.broadcasted_iota(jnp.int32, (rows, 128), 0)
    own = row[:PANEL]
    columns = [jnp.broadcast_to(right[:, at + j:at + j + 1], (rows, 128)) for j in range(PANEL)]
    pivots = jnp.ones((PANEL, 128), F32)
    for j in range(0, PANEL, 2):
        c0, c1 = columns[j], columns[j + 1]
        a, b, c = c0[j:j + 1], c1[j:j + 1], c1[j + 1:j + 2]
        det = a * c - b * b
        inv_a, inv_det = 1.0 / a, 1.0 / det
        pivots = jnp.where(own == j, a, jnp.where(own == j + 1, det * inv_a, pivots))
        below = row > j + 1
        g0 = jnp.where(below, (c0 * c - c1 * b) * inv_det, jnp.where(row == j + 1, b * inv_a, 0.0))
        g1 = jnp.where(below, (c1 * a - c0 * b) * inv_det, 0.0)
        for m in range(j + 2, PANEL):
            columns[m] = columns[m] - g0 * columns[m][j:j + 1] - g1 * columns[m][j + 1:j + 2]
        right = right - wide(g0, width) * right[j:j + 1] - wide(g1, width) * right[j + 1:j + 2]
        left = left - wide(g0, reach) * left[j:j + 1] - wide(g1, reach) * left[j + 1:j + 2]
    scale = lax.rsqrt(pivots)
    done = right[:PANEL] * wide(scale, width), left[:PANEL] * wide(scale, reach)
    return done, right[PANEL:], left[PANEL:]


def invert_factor(gram, inverse):
    n = gram.shape[0]
    for k in range(0, n, WINDOW):
        end = k + WINDOW
        start, reach = k // 128 * 128, -(-end // 128) * 128
        right, left = gram[k:end, start:n], inverse[k:end, :reach]
        done = []
        for first in range(0, WINDOW, PANEL):
            panel, right, left = eliminate_panel(right, left, k - start + first)
            done.append(panel)
        right, left = (jnp.concatenate(part, 0) for part in zip(*done, strict=True))
        inverse[k:end, :reach] = left
        if end < n:
            base = end // 128 * 128
            rest = right[:, base - start:]
            change = transposed_dot(rest, jnp.concatenate([rest, left], 1))[end - base:]
            gram[end:n, base:n] -= change[:, :n - base]
            inverse[end:n, :reach] -= change[:, n - base:]


def basis_kernel(pixels, pix_ref, mine_ref, other_ref, *refs):
    pieces, (basis_ref, gram, inverse) = refs[:-3], refs[-3:]
    n = gram.shape[0]
    half = n // 2
    first = pix_ref[0] == 0
    mine, other = mine_ref[...], other_ref[...]
    above = jnp.where(first, mine[:half], other[:half])
    both = jnp.where(first, other, mine)
    row = lax.broadcasted_iota(jnp.int32, (half, half), 0)
    col = lax.broadcasted_iota(jnp.int32, (half, half), 1)
    eye = row == col
    both, corner = both[:half], both[half:half + 1]
    turned = both.T
    blocks = [jnp.where(row >= col, both, turned), jnp.where(eye, corner, jnp.where(row > col, turned, both))]
    across = [lax.rsqrt(jnp.sum(jnp.where(eye, blk, 0.0), 0, keepdims=True)) for blk in blocks]
    down = [lax.rsqrt(jnp.sum(jnp.where(eye, blk, 0.0), 1, keepdims=True)) for blk in blocks]
    gram[:half, :half] = blocks[0] * across[0] * down[0]
    gram[:half, half:] = above * across[1] * down[0]
    gram[half:, half:] = blocks[1] * across[1] * down[1]
    zero = jnp.zeros((half, half), F32)
    root = math.sqrt(pixels)
    inverse[:half, :half] = jnp.where(eye, jnp.broadcast_to(across[0] * root, (half, half)), 0.0)
    inverse[half:, half:] = jnp.where(eye, jnp.broadcast_to(across[1] * root, (half, half)), 0.0)
    inverse[:half, half:] = zero
    inverse[half:, :half] = zero
    invert_factor(gram, inverse)
    rows = 0
    for x in pieces:
        basis_ref[rows:rows + x.shape[0]] = lax.dot_general(
            x[...], inverse[...], (((1,), (1,)), ((), ())),
            precision=lax.Precision.HIGHEST, preferred_element_type=F32,
        )
        rows += x.shape[0]


def basis_of(pix, mine, other, image, pixels):
    cols = image[0].shape[1]
    rows = sum(x.shape[0] for x in image)
    return pl.pallas_call(
        functools.partial(basis_kernel, pixels),
        in_specs=[SMEM] + [VMEM] * (2 + len(image)),
        out_specs=VMEM,
        out_shape=jax.ShapeDtypeStruct((rows, cols), F32),
        scratch_shapes=[pltpu.VMEM((cols, cols), F32)] * 2,
        compiler_params=params(),
    )(pix, mine, other, *image)


def split(rows):
    ends = [-(-rows // 16 * sum(SHARES[:k]) // sum(SHARES)) * 16 for k in range(len(SHARES) + 1)]
    return [last - first for first, last in zip(ends, ends[1:]) if last > first]


def xor_pairs(n, d):
    return [(i, i ^ d) for i in range(n)]


def on_device(n_bins, spectra, probes):
    rows_dev, bins = spectra.shape
    cols = probes.shape[1]
    rows = rows_dev // n_bins
    me = lax.axis_index("bins")
    pix = lax.axis_index("pix").astype(jnp.int32).reshape(1)
    idx = jnp.stack([me % 2, me // 2]).astype(jnp.int32)

    sizes = split(rows)
    terms = loadings_terms(spectra, probes)
    got = lax.ppermute(terms, "pix", xor_pairs(2, 1))
    blocks = fetch_blocks(idx, spectra, rows, terms)
    loadings, *away = image_away(blocks, terms, got, sizes)
    away = [lax.ppermute(out, "bins", xor_pairs(n_bins, 1)) for out in away]
    kept = image_kept(idx, spectra, loadings, sizes)
    gram = jnp.zeros((cols, cols), F32)
    image = []
    for c in range(len(sizes)):
        own, *sends = add_chunk(idx, away[c], kept[c], image[c - 2:c - 1] if c > 1 else [])
        arrived = [lax.ppermute(s, "bins", xor_pairs(n_bins, 2 * (d + 1))) for d, s in enumerate(sends)]
        if c < len(sizes) - 1:
            x, gram = gram_chunk(own, arrived, gram)
        else:
            x, mine, other = gram_chunk(own, arrived, gram, pix)
        image.append(x)

    mine = mine + lax.ppermute(other, "pix", xor_pairs(2, 1))
    d = 1
    while d < n_bins:
        mine = mine + lax.ppermute(mine, "bins", xor_pairs(n_bins, d))
        d *= 2
    other = lax.ppermute(mine, "pix", xor_pairs(2, 1))
    basis = basis_of(pix, mine, other, image, 2 * rows_dev)
    return basis.reshape(1, rows, cols)


def solution(mesh):
    return jax.shard_map(
        functools.partial(on_device, mesh.shape["bins"]),
        mesh=mesh,
        in_specs=(P(("parts", "pix"), "bins"), P(("parts", "pix"), None)),
        out_specs=P(("parts", "pix"), "bins", None),
        check_vma=False,
    )
```

```python
import functools
import math
import jax
import jax.numpy as jnp
from jax import lax
from jax.experimental import pallas as pl
from jax.experimental.pallas import tpu as pltpu
from jax.sharding import PartitionSpec as P

SHARES = (13, 13, 6)
PIECES = 8
PANEL = 16
WINDOW = 32
F32 = jnp.float32
BF16 = jnp.bfloat16
MIB = 1 << 20
VMEM = pl.BlockSpec(memory_space=pltpu.VMEM)
SMEM = pl.BlockSpec(memory_space=pltpu.SMEM)
HBM = pl.BlockSpec(memory_space=pltpu.HBM)


def params(mib=32):
    return pltpu.CompilerParams(vmem_limit_bytes=mib * MIB)


def loadings_kernel(spectra_hbm, probes_hbm, terms_ref, spectra_ref, probes_ref, sems):
    rows = spectra_ref.shape[0] // PIECES

    def copies(i):
        part = pl.ds(i * rows, rows)
        return (
            pltpu.make_async_copy(probes_hbm.at[part], probes_ref.at[part], sems.at[0, i]),
            pltpu.make_async_copy(spectra_hbm.at[part], spectra_ref.at[part], sems.at[1, i]),
        )

    for i in range(PIECES):
        for copy in copies(i):
            copy.start()
    for i in range(PIECES):
        for copy in copies(i):
            copy.wait()
        part = pl.ds(i * rows, rows)
        term = lax.dot_general(
            probes_ref[part], spectra_ref[part], (((0,), (0,)), ((), ())), preferred_element_type=F32
        )
        if i == 0:
            terms_ref[...] = term
        else:
            terms_ref[...] += term


def loadings_terms(spectra, probes):
    rows, bins = spectra.shape
    cols = probes.shape[1]
    return pl.pallas_call(
        loadings_kernel,
        in_specs=[HBM, HBM],
        out_specs=VMEM,
        out_shape=jax.ShapeDtypeStruct((cols, bins), F32),
        scratch_shapes=[
            pltpu.VMEM((rows, bins), BF16),
            pltpu.VMEM((rows, cols), BF16),
            pltpu.SemaphoreType.DMA((2, PIECES)),
        ],
        compiler_params=params(51),
        cost_estimate=pl.CostEstimate(
            flops=2 * rows * bins * cols, bytes_accessed=rows * (bins + cols) * 2, transcendentals=0
        ),
    )(spectra, probes)


def block_copies(spectra_hbm, target_ref, sems, sources, size):
    return [
        pltpu.make_async_copy(
            spectra_hbm.at[pl.ds(pl.multiple_of(start, 16), size)], target_ref.at[pl.ds(i * size, size)], sems.at[i]
        )
        for i, start in enumerate(sources)
    ]


def fetch_kernel(sizes, idx_ref, spectra_hbm, after_ref, *refs):
    *targets, sems = refs
    rows, outer = sum(sizes), spectra_hbm.shape[0] // (2 * sum(sizes))
    side, me = idx_ref[0], idx_ref[1]
    copies, first = [], 0
    for c, size in enumerate(sizes):
        if c < len(sizes) - 1:
            sources = [(i * 2 + 1 - side) * rows + first for i in range(outer)]
        else:
            sources = [
                (lax.bitwise_xor(me, d) * 2 + y) * rows + first for d in range(outer) for y in (side, 1 - side)
            ]
        copies += block_copies(spectra_hbm, targets[c], sems.at[c], sources, size)
        first += size
    for copy in copies:
        copy.start()
    for copy in copies:
        copy.wait()


def fetch_blocks(idx, spectra, sizes, after):
    outer, bins = spectra.shape[0] // (2 * sum(sizes)), spectra.shape[1]
    heights = [outer * size for size in sizes[:-1]] + [2 * outer * sizes[-1]]
    return pl.pallas_call(
        functools.partial(fetch_kernel, sizes),
        in_specs=[SMEM, HBM, pl.BlockSpec(memory_space=pl.ANY)],
        out_specs=[VMEM] * len(sizes),
        out_shape=[jax.ShapeDtypeStruct((height, bins), BF16) for height in heights],
        scratch_shapes=[pltpu.SemaphoreType.DMA((len(sizes), 2 * outer))],
        compiler_params=params(46),
        cost_estimate=pl.CostEstimate(flops=0, bytes_accessed=sum(heights) * bins * 4, transcendentals=0),
    )(idx, spectra, after)


def away_kernel(n, *refs):
    blocks, (mine_ref, got_ref, loadings_ref, *outs) = refs[:n], refs[n:]
    loadings_ref[...] = (mine_ref[...] + got_ref[...]).T.astype(BF16)
    products = [jnp.dot(x[...], loadings_ref[...], preferred_element_type=F32) for x in blocks]
    for product, out_ref in zip(products[:-1], outs):
        out_ref[...] = product.astype(BF16)
    size = outs[-1].shape[0]
    for d, out_ref in enumerate(outs[n - 1:]):
        out_ref[...] = products[-1][d * size:(d + 1) * size].astype(out_ref.dtype)


def image_away(blocks, mine, got, outer):
    cols, bins = mine.shape
    size = blocks[-1].shape[0] // outer
    shapes = [jax.ShapeDtypeStruct((bins, cols), BF16)]
    shapes += [jax.ShapeDtypeStruct((x.shape[0], cols), BF16) for x in blocks[:-1]]
    shapes += [jax.ShapeDtypeStruct((size, cols), BF16 if d else F32) for d in range(outer)]
    height = sum(x.shape[0] for x in blocks)
    return pl.pallas_call(
        functools.partial(away_kernel, len(blocks)),
        in_specs=[VMEM] * (len(blocks) + 2),
        out_specs=[VMEM] * len(shapes),
        out_shape=shapes,
        compiler_params=params(),
        cost_estimate=pl.CostEstimate(
            flops=2 * height * bins * cols, bytes_accessed=height * cols * 4, transcendentals=0
        ),
    )(*blocks, mine, got)


def kept_kernel(rows, sizes, idx_ref, spectra_hbm, loadings_ref, *refs):
    outs, (blocks_ref, sems) = refs[:-2], refs[-2:]
    outer, size = blocks_ref.shape[0] // sum(sizes), sum(sizes)
    copies = block_copies(
        spectra_hbm, blocks_ref, sems, [(i * 2 + idx_ref[0]) * rows for i in range(outer)], size
    )
    for copy in copies:
        copy.start()
    for i, copy in enumerate(copies):
        copy.wait()
        product = jnp.dot(blocks_ref[i * size:(i + 1) * size], loadings_ref[...], preferred_element_type=F32)
        first = 0
        for out_ref in outs:
            out_ref[i] = product[first:first + out_ref.shape[1]]
            first += out_ref.shape[1]


def image_kept(idx, spectra, loadings, rows, sizes):
    outer, (bins, cols) = spectra.shape[0] // (2 * rows), loadings.shape
    return pl.pallas_call(
        functools.partial(kept_kernel, rows, sizes),
        in_specs=[SMEM, HBM, VMEM],
        out_specs=[VMEM] * len(sizes),
        out_shape=[jax.ShapeDtypeStruct((outer, size, cols), F32) for size in sizes],
        scratch_shapes=[pltpu.VMEM((outer * sum(sizes), bins), BF16), pltpu.SemaphoreType.DMA((outer,))],
        compiler_params=params(48),
        cost_estimate=pl.CostEstimate(
            flops=2 * outer * rows * bins * cols, bytes_accessed=outer * rows * (bins * 2 + cols * 4), transcendentals=0
        ),
    )(idx, spectra, loadings)


def sides_kernel(mine_ref, *refs):
    *got_refs, own_ref, send_ref = refs
    total = mine_ref[...]
    for got in got_refs:
        total = total + got[...].astype(F32)
    size = own_ref.shape[0]
    own_ref[...] = total[:size]
    send_ref[...] = total[size:].astype(BF16)


def sides_chunk(mine, got):
    size, cols = mine.shape[0] // 2, mine.shape[1]
    return pl.pallas_call(
        sides_kernel,
        in_specs=[VMEM] * (1 + len(got)),
        out_specs=[VMEM] * 2,
        out_shape=[jax.ShapeDtypeStruct((size, cols), F32), jax.ShapeDtypeStruct((size, cols), BF16)],
        compiler_params=params(),
        cost_estimate=pl.CostEstimate(flops=8 * size * cols, bytes_accessed=16 * size * cols, transcendentals=0),
    )(mine, *got)


def add_kernel(n_after, idx_ref, got_ref, kept_ref, *refs):
    own_ref, *send_refs = refs[n_after:]
    me = idx_ref[1]
    own_ref[...] = got_ref[me].astype(F32) + kept_ref[me]
    for d, send in enumerate(send_refs):
        other = lax.bitwise_xor(me, d + 1)
        send[...] = (got_ref[other].astype(F32) + kept_ref[other]).astype(send.dtype)


def add_chunk(idx, got, kept, after):
    outer, piece, cols = got.shape
    return pl.pallas_call(
        functools.partial(add_kernel, len(after)),
        in_specs=[SMEM, VMEM, VMEM] + [pl.BlockSpec(memory_space=pl.ANY)] * len(after),
        out_specs=[VMEM] * outer,
        out_shape=[jax.ShapeDtypeStruct((piece, cols), F32)]
        + [jax.ShapeDtypeStruct((piece, cols), BF16)] * (outer - 1),
        compiler_params=params(),
        cost_estimate=pl.CostEstimate(
            flops=outer * piece * cols, bytes_accessed=outer * piece * cols * 8, transcendentals=0
        ),
    )(idx, got, kept, *after)


def gram_kernel(n, last, *refs):
    if last:
        pix_ref, refs = refs[0], refs[1:]
    own_ref, got, (gram_in, x_ref, *out) = refs[0], refs[1:n], refs[n:]
    x = own_ref[...]
    for g in got:
        x = x + g[...].astype(F32)
    x_ref[...] = x
    gram = gram_in[...] + lax.dot_general(
        x, x, (((0,), (0,)), ((), ())), precision=lax.Precision.HIGHEST, preferred_element_type=F32
    )
    if not last:
        out[0][...] = gram
        return
    half = gram.shape[0] // 2
    mine, other = out
    row = lax.broadcasted_iota(jnp.int32, (half, half), 0)
    col = lax.broadcasted_iota(jnp.int32, (half, half), 1)
    corner = gram[half:, half:]
    diag = jnp.sum(jnp.where(row == col, corner, 0.0), 0, keepdims=True)
    above = gram[:half, half:]
    both = jnp.where(row >= col, gram[:half, :half], corner)
    first = pix_ref[0] == 0
    mine[:half] = jnp.where(first, above, both)
    other[:half] = jnp.where(first, both, above)
    mine[half:] = jnp.broadcast_to(diag, (8, half))
    other[half:] = jnp.broadcast_to(diag, (8, half))


def gram_chunk(own, got, gram, pix=None):
    piece, cols = own.shape
    n = 1 + len(got)
    half = cols // 2
    last = pix is not None
    shapes = [(half + 8, half)] * 2 if last else [(cols, cols)]
    return pl.pallas_call(
        functools.partial(gram_kernel, n, last),
        in_specs=[SMEM] * last + [VMEM] * (n + 1),
        out_specs=[VMEM] * (1 + len(shapes)),
        out_shape=[jax.ShapeDtypeStruct(s, F32) for s in [(piece, cols)] + shapes],
        compiler_params=params(),
        cost_estimate=pl.CostEstimate(
            flops=12 * piece * cols * cols, bytes_accessed=n * piece * cols * 4, transcendentals=0
        ),
    )(*[pix] * last, own, *got, gram)


def transposed_dot(a, b):
    def terms(x):
        high = x.astype(BF16)
        rest = x - high.astype(F32)
        middle = rest.astype(BF16)
        return high, middle, (rest - middle.astype(F32)).astype(BF16)

    (a0, a1, a2), (b0, b1, b2) = terms(a), terms(b)
    return lax.dot_general(
        jnp.concatenate([a0, a0, a1, a1, a0, a2], 0), jnp.concatenate([b0, b1, b0, b1, b2, b0], 0),
        (((0,), (0,)), ((), ())), preferred_element_type=F32,
    )


def wide(column, width):
    return column if width == 128 else jnp.concatenate([column] * (width // 128), 1)


def eliminate_panel(right, left, at):
    rows, width = right.shape
    reach = left.shape[1]
    row = lax.broadcasted_iota(jnp.int32, (rows, 128), 0)
    own = row[:PANEL]
    columns = [jnp.broadcast_to(right[:, at + j:at + j + 1], (rows, 128)) for j in range(PANEL)]
    pivots = jnp.ones((PANEL, 128), F32)
    for j in range(0, PANEL, 2):
        c0, c1 = columns[j], columns[j + 1]
        a, b, c = c0[j:j + 1], c1[j:j + 1], c1[j + 1:j + 2]
        det = a * c - b * b
        inv_a, inv_det = 1.0 / a, 1.0 / det
        pivots = jnp.where(own == j, a, jnp.where(own == j + 1, det * inv_a, pivots))
        below = row > j + 1
        g0 = jnp.where(below, (c0 * c - c1 * b) * inv_det, jnp.where(row == j + 1, b * inv_a, 0.0))
        g1 = jnp.where(below, (c1 * a - c0 * b) * inv_det, 0.0)
        for m in range(j + 2, PANEL):
            columns[m] = columns[m] - g0 * columns[m][j:j + 1] - g1 * columns[m][j + 1:j + 2]
        right = right - wide(g0, width) * right[j:j + 1] - wide(g1, width) * right[j + 1:j + 2]
        left = left - wide(g0, reach) * left[j:j + 1] - wide(g1, reach) * left[j + 1:j + 2]
    scale = lax.rsqrt(pivots)
    done = right[:PANEL] * wide(scale, width), left[:PANEL] * wide(scale, reach)
    return done, right[PANEL:], left[PANEL:]


def invert_factor(gram, inverse):
    n = gram.shape[0]
    for k in range(0, n, WINDOW):
        end = k + WINDOW
        start, reach = k // 128 * 128, -(-end // 128) * 128
        right, left = gram[k:end, start:n], inverse[k:end, :reach]
        done = []
        for first in range(0, WINDOW, PANEL):
            panel, right, left = eliminate_panel(right, left, k - start + first)
            done.append(panel)
        right, left = (jnp.concatenate(part, 0) for part in zip(*done, strict=True))
        inverse[k:end, :reach] = left
        if end < n:
            base = end // 128 * 128
            rest = right[:, base - start:]
            change = transposed_dot(rest, jnp.concatenate([rest, left], 1))[end - base:]
            gram[end:n, base:n] -= change[:, :n - base]
            inverse[end:n, :reach] -= change[:, n - base:]


def basis_kernel(pixels, pix_ref, mine_ref, other_ref, *refs):
    pieces, (basis_ref, gram, inverse) = refs[:-3], refs[-3:]
    n = gram.shape[0]
    half = n // 2
    first = pix_ref[0] == 0
    mine, other = mine_ref[...], other_ref[...]
    above = jnp.where(first, mine[:half], other[:half])
    both = jnp.where(first, other, mine)
    row = lax.broadcasted_iota(jnp.int32, (half, half), 0)
    col = lax.broadcasted_iota(jnp.int32, (half, half), 1)
    eye = row == col
    both, corner = both[:half], both[half:half + 1]
    turned = both.T
    blocks = [jnp.where(row >= col, both, turned), jnp.where(eye, corner, jnp.where(row > col, turned, both))]
    across = [lax.rsqrt(jnp.sum(jnp.where(eye, blk, 0.0), 0, keepdims=True)) for blk in blocks]
    down = [lax.rsqrt(jnp.sum(jnp.where(eye, blk, 0.0), 1, keepdims=True)) for blk in blocks]
    gram[:half, :half] = blocks[0] * across[0] * down[0]
    gram[:half, half:] = above * across[1] * down[0]
    gram[half:, half:] = blocks[1] * across[1] * down[1]
    zero = jnp.zeros((half, half), F32)
    root = math.sqrt(pixels)
    inverse[:half, :half] = jnp.where(eye, jnp.broadcast_to(across[0] * root, (half, half)), 0.0)
    inverse[half:, half:] = jnp.where(eye, jnp.broadcast_to(across[1] * root, (half, half)), 0.0)
    inverse[:half, half:] = zero
    inverse[half:, :half] = zero
    invert_factor(gram, inverse)
    rows = 0
    for x in pieces:
        basis_ref[rows:rows + x.shape[0]] = lax.dot_general(
            x[...], inverse[...], (((1,), (1,)), ((), ())),
            precision=lax.Precision.HIGHEST, preferred_element_type=F32,
        )
        rows += x.shape[0]


def basis_of(pix, mine, other, image, pixels):
    cols = image[0].shape[1]
    rows = sum(x.shape[0] for x in image)
    return pl.pallas_call(
        functools.partial(basis_kernel, pixels),
        in_specs=[SMEM] + [VMEM] * (2 + len(image)),
        out_specs=VMEM,
        out_shape=jax.ShapeDtypeStruct((rows, cols), F32),
        scratch_shapes=[pltpu.VMEM((cols, cols), F32)] * 2,
        compiler_params=params(),
    )(pix, mine, other, *image)


def split(rows):
    ends = [-(-rows // 16 * sum(SHARES[:k]) // sum(SHARES)) * 16 for k in range(len(SHARES) + 1)]
    return [last - first for first, last in zip(ends, ends[1:]) if last > first]


def xor_pairs(n, d):
    return [(i, i ^ d) for i in range(n)]


def on_device(n_bins, spectra, probes):
    rows_dev, bins = spectra.shape
    cols = probes.shape[1]
    rows = rows_dev // n_bins
    me = lax.axis_index("bins")
    pix = lax.axis_index("pix").astype(jnp.int32).reshape(1)
    idx = jnp.stack([me % 2, me // 2]).astype(jnp.int32)

    sizes = split(rows)
    terms = loadings_terms(spectra, probes)
    got = lax.ppermute(terms, "pix", xor_pairs(2, 1))
    outer = n_bins // 2
    blocks = fetch_blocks(idx, spectra, sizes, terms)
    loadings, *parts = image_away(blocks, terms, got, outer)
    n = len(sizes) - 1
    away = [
        lax.ppermute(out.reshape(outer, -1, cols), "bins", xor_pairs(n_bins, 1)) for out in parts[:n]
    ]

    def along_z(sends):
        return [
            lax.ppermute(sends[d - 1], "bins", xor_pairs(n_bins, 2 * d)) for d in range(outer - 1, 0, -1)
        ]

    sides = along_z(parts[n + 1:])
    kept = image_kept(idx, spectra, loadings, rows, sizes[:-1])
    gram = jnp.zeros((cols, cols), F32)
    own, send = sides_chunk(parts[n], sides)
    crossed = lax.ppermute(send, "bins", xor_pairs(n_bins, 1))
    last, gram = gram_chunk(own, [crossed], gram)
    image = []
    for c in range(n):
        first, *sends = add_chunk(idx, away[c], kept[c], [own] if c == 0 else [])
        arrived = along_z(sends)
        if c < n - 1:
            x, gram = gram_chunk(first, arrived, gram)
        else:
            x, mine, other = gram_chunk(first, arrived, gram, pix)
        image.append(x)
    image.append(last)

    mine = mine + lax.ppermute(other, "pix", xor_pairs(2, 1))
    d = 1
    while d < n_bins:
        if d == 1 and n_bins > 2:
            both, near, far = (lax.ppermute(mine, "bins", xor_pairs(n_bins, k)) for k in (3, 1, 2))
            mine, d = (mine + near) + (far + both), 4
        else:
            mine, d = mine + lax.ppermute(mine, "bins", xor_pairs(n_bins, d)), 2 * d
    other = lax.ppermute(mine, "pix", xor_pairs(2, 1))
    basis = basis_of(pix, mine, other, image, 2 * rows_dev)
    return basis.reshape(1, rows, cols)


def solution(mesh):
    return jax.shard_map(
        functools.partial(on_device, mesh.shape["bins"]),
        mesh=mesh,
        in_specs=(P(("parts", "pix"), "bins"), P(("parts", "pix"), None)),
        out_specs=P(("parts", "pix"), "bins", None),
        check_vma=False,
    )
```

```python
import functools
import math
import jax
import jax.numpy as jnp
from jax import lax
from jax.experimental import pallas as pl
from jax.experimental.pallas import tpu as pltpu
from jax.sharding import PartitionSpec as P

SHARES = (13, 12, 7)
PIECES = 8
PANEL = 16
WINDOW = 32
F32 = jnp.float32
BF16 = jnp.bfloat16
MIB = 1 << 20
VMEM = pl.BlockSpec(memory_space=pltpu.VMEM)
SMEM = pl.BlockSpec(memory_space=pltpu.SMEM)
HBM = pl.BlockSpec(memory_space=pltpu.HBM)


def params(mib=32):
    return pltpu.CompilerParams(vmem_limit_bytes=mib * MIB)


def loadings_kernel(spectra_hbm, probes_hbm, terms_ref, spectra_ref, probes_ref, sems):
    rows = spectra_ref.shape[0] // PIECES

    def copies(i):
        part = pl.ds(i * rows, rows)
        return (
            pltpu.make_async_copy(probes_hbm.at[part], probes_ref.at[part], sems.at[0, i]),
            pltpu.make_async_copy(spectra_hbm.at[part], spectra_ref.at[part], sems.at[1, i]),
        )

    for i in range(PIECES):
        for copy in copies(i):
            copy.start()
    for i in range(PIECES):
        for copy in copies(i):
            copy.wait()
        part = pl.ds(i * rows, rows)
        term = lax.dot_general(
            probes_ref[part], spectra_ref[part], (((0,), (0,)), ((), ())), preferred_element_type=F32
        )
        if i == 0:
            terms_ref[...] = term
        else:
            terms_ref[...] += term


def loadings_terms(spectra, probes):
    rows, bins = spectra.shape
    cols = probes.shape[1]
    return pl.pallas_call(
        loadings_kernel,
        in_specs=[HBM, HBM],
        out_specs=VMEM,
        out_shape=jax.ShapeDtypeStruct((cols, bins), F32),
        scratch_shapes=[
            pltpu.VMEM((rows, bins), BF16),
            pltpu.VMEM((rows, cols), BF16),
            pltpu.SemaphoreType.DMA((2, PIECES)),
        ],
        compiler_params=params(51),
        cost_estimate=pl.CostEstimate(
            flops=2 * rows * bins * cols, bytes_accessed=rows * (bins + cols) * 2, transcendentals=0
        ),
    )(spectra, probes)


def block_copies(spectra_hbm, target_ref, sems, sources, size):
    return [
        pltpu.make_async_copy(
            spectra_hbm.at[pl.ds(pl.multiple_of(start, 16), size)], target_ref.at[pl.ds(i * size, size)], sems.at[i]
        )
        for i, start in enumerate(sources)
    ]


def fetch_kernel(sizes, idx_ref, spectra_hbm, after_ref, *refs):
    *targets, sems = refs
    rows, outer = sum(sizes), spectra_hbm.shape[0] // (2 * sum(sizes))
    side, me = idx_ref[0], idx_ref[1]
    copies, first = [], 0
    for c, size in enumerate(sizes):
        if c < len(sizes) - 1:
            sources = [(i * 2 + 1 - side) * rows + first for i in range(outer)]
        else:
            sources = [
                (lax.bitwise_xor(me, d) * 2 + y) * rows + first for d in range(outer) for y in (side, 1 - side)
            ]
        copies += block_copies(spectra_hbm, targets[c], sems.at[c], sources, size)
        first += size
    for copy in copies:
        copy.start()
    for copy in copies:
        copy.wait()


def fetch_blocks(idx, spectra, sizes, after):
    outer, bins = spectra.shape[0] // (2 * sum(sizes)), spectra.shape[1]
    heights = [outer * size for size in sizes[:-1]] + [2 * outer * sizes[-1]]
    return pl.pallas_call(
        functools.partial(fetch_kernel, sizes),
        in_specs=[SMEM, HBM, pl.BlockSpec(memory_space=pl.ANY)],
        out_specs=[VMEM] * len(sizes),
        out_shape=[jax.ShapeDtypeStruct((height, bins), BF16) for height in heights],
        scratch_shapes=[pltpu.SemaphoreType.DMA((len(sizes), 2 * outer))],
        compiler_params=params(46),
        cost_estimate=pl.CostEstimate(flops=0, bytes_accessed=sum(heights) * bins * 4, transcendentals=0),
    )(idx, spectra, after)


def away_kernel(n, *refs):
    blocks, (mine_ref, got_ref, loadings_ref, *outs) = refs[:n], refs[n:]
    loadings_ref[...] = (mine_ref[...] + got_ref[...]).T.astype(BF16)
    products = [jnp.dot(x[...], loadings_ref[...], preferred_element_type=F32) for x in blocks]
    for product, out_ref in zip(products[:-1], outs):
        out_ref[...] = product.astype(BF16)
    size = outs[-1].shape[0]
    for d, out_ref in enumerate(outs[n - 1:]):
        out_ref[...] = products[-1][d * size:(d + 1) * size].astype(out_ref.dtype)


def image_away(blocks, mine, got, outer):
    cols, bins = mine.shape
    size = blocks[-1].shape[0] // outer
    shapes = [jax.ShapeDtypeStruct((bins, cols), BF16)]
    shapes += [jax.ShapeDtypeStruct((x.shape[0], cols), BF16) for x in blocks[:-1]]
    shapes += [jax.ShapeDtypeStruct((size, cols), BF16 if d else F32) for d in range(outer)]
    height = sum(x.shape[0] for x in blocks)
    return pl.pallas_call(
        functools.partial(away_kernel, len(blocks)),
        in_specs=[VMEM] * (len(blocks) + 2),
        out_specs=[VMEM] * len(shapes),
        out_shape=shapes,
        compiler_params=params(),
        cost_estimate=pl.CostEstimate(
            flops=2 * height * bins * cols, bytes_accessed=height * cols * 4, transcendentals=0
        ),
    )(*blocks, mine, got)


def kept_kernel(rows, sizes, idx_ref, spectra_hbm, loadings_ref, *refs):
    outs, (blocks_ref, sems) = refs[:-2], refs[-2:]
    outer, size = blocks_ref.shape[0] // sum(sizes), sum(sizes)
    copies = block_copies(
        spectra_hbm, blocks_ref, sems, [(i * 2 + idx_ref[0]) * rows for i in range(outer)], size
    )
    for copy in copies:
        copy.start()
    for i, copy in enumerate(copies):
        copy.wait()
        product = jnp.dot(blocks_ref[i * size:(i + 1) * size], loadings_ref[...], preferred_element_type=F32)
        first = 0
        for out_ref in outs:
            out_ref[i] = product[first:first + out_ref.shape[1]]
            first += out_ref.shape[1]


def image_kept(idx, spectra, loadings, rows, sizes):
    outer, (bins, cols) = spectra.shape[0] // (2 * rows), loadings.shape
    return pl.pallas_call(
        functools.partial(kept_kernel, rows, sizes),
        in_specs=[SMEM, HBM, VMEM],
        out_specs=[VMEM] * len(sizes),
        out_shape=[jax.ShapeDtypeStruct((outer, size, cols), F32) for size in sizes],
        scratch_shapes=[pltpu.VMEM((outer * sum(sizes), bins), BF16), pltpu.SemaphoreType.DMA((outer,))],
        compiler_params=params(48),
        cost_estimate=pl.CostEstimate(
            flops=2 * outer * rows * bins * cols, bytes_accessed=outer * rows * (bins * 2 + cols * 4), transcendentals=0
        ),
    )(idx, spectra, loadings)


def sides_kernel(mine_ref, *refs):
    *got_refs, own_ref, send_ref = refs
    total = mine_ref[...]
    for got in got_refs:
        total = total + got[...].astype(F32)
    size = own_ref.shape[0]
    own_ref[...] = total[:size]
    send_ref[...] = total[size:].astype(BF16)


def sides_chunk(mine, got):
    size, cols = mine.shape[0] // 2, mine.shape[1]
    return pl.pallas_call(
        sides_kernel,
        in_specs=[VMEM] * (1 + len(got)),
        out_specs=[VMEM] * 2,
        out_shape=[jax.ShapeDtypeStruct((size, cols), F32), jax.ShapeDtypeStruct((size, cols), BF16)],
        compiler_params=params(),
        cost_estimate=pl.CostEstimate(flops=8 * size * cols, bytes_accessed=16 * size * cols, transcendentals=0),
    )(mine, *got)


def add_kernel(idx_ref, got_ref, kept_ref, own_ref, *send_refs):
    me = idx_ref[1]
    own_ref[...] = got_ref[me].astype(F32) + kept_ref[me]
    for d, send in enumerate(send_refs):
        other = lax.bitwise_xor(me, d + 1)
        send[...] = (got_ref[other].astype(F32) + kept_ref[other]).astype(send.dtype)


def add_chunk(idx, got, kept):
    outer, piece, cols = got.shape
    return pl.pallas_call(
        add_kernel,
        in_specs=[SMEM, VMEM, VMEM],
        out_specs=[VMEM] * outer,
        out_shape=[jax.ShapeDtypeStruct((piece, cols), F32)]
        + [jax.ShapeDtypeStruct((piece, cols), BF16)] * (outer - 1),
        compiler_params=params(),
        cost_estimate=pl.CostEstimate(
            flops=outer * piece * cols, bytes_accessed=outer * piece * cols * 8, transcendentals=0
        ),
    )(idx, got, kept)


def gram_kernel(n, last, *refs):
    if last:
        pix_ref, refs = refs[0], refs[1:]
    own_ref, got, (gram_in, x_ref, *out) = refs[0], refs[1:n], refs[n:]
    x = own_ref[...]
    for g in got:
        x = x + g[...].astype(F32)
    x_ref[...] = x
    gram = gram_in[...] + lax.dot_general(
        x, x, (((0,), (0,)), ((), ())), precision=lax.Precision.HIGHEST, preferred_element_type=F32
    )
    if not last:
        out[0][...] = gram
        return
    half = gram.shape[0] // 2
    mine, other = out
    row = lax.broadcasted_iota(jnp.int32, (half, half), 0)
    col = lax.broadcasted_iota(jnp.int32, (half, half), 1)
    corner = gram[half:, half:]
    diag = jnp.sum(jnp.where(row == col, corner, 0.0), 0, keepdims=True)
    above = gram[:half, half:]
    both = jnp.where(row >= col, gram[:half, :half], corner)
    first = pix_ref[0] == 0
    mine[:half] = jnp.where(first, above, both)
    other[:half] = jnp.where(first, both, above)
    mine[half:] = jnp.broadcast_to(diag, (8, half))
    other[half:] = jnp.broadcast_to(diag, (8, half))


def gram_chunk(own, got, gram, pix=None):
    piece, cols = own.shape
    n = 1 + len(got)
    half = cols // 2
    last = pix is not None
    shapes = [(half + 8, half)] * 2 if last else [(cols, cols)]
    return pl.pallas_call(
        functools.partial(gram_kernel, n, last),
        in_specs=[SMEM] * last + [VMEM] * (n + 1),
        out_specs=[VMEM] * (1 + len(shapes)),
        out_shape=[jax.ShapeDtypeStruct(s, F32) for s in [(piece, cols)] + shapes],
        compiler_params=params(),
        cost_estimate=pl.CostEstimate(
            flops=12 * piece * cols * cols, bytes_accessed=n * piece * cols * 4, transcendentals=0
        ),
    )(*[pix] * last, own, *got, gram)


def transposed_dot(a, b):
    def terms(x):
        high = x.astype(BF16)
        rest = x - high.astype(F32)
        middle = rest.astype(BF16)
        return high, middle, (rest - middle.astype(F32)).astype(BF16)

    (a0, a1, a2), (b0, b1, b2) = terms(a), terms(b)
    return lax.dot_general(
        jnp.concatenate([a0, a0, a1, a1, a0, a2], 0), jnp.concatenate([b0, b1, b0, b1, b2, b0], 0),
        (((0,), (0,)), ((), ())), preferred_element_type=F32,
    )


def wide(column, width):
    return column if width == 128 else jnp.concatenate([column] * (width // 128), 1)


def eliminate_panel(right, left, at):
    rows, width = right.shape
    reach = left.shape[1]
    row = lax.broadcasted_iota(jnp.int32, (rows, 128), 0)
    own = row[:PANEL]
    columns = [jnp.broadcast_to(right[:, at + j:at + j + 1], (rows, 128)) for j in range(PANEL)]
    pivots = jnp.ones((PANEL, 128), F32)
    for j in range(0, PANEL, 2):
        c0, c1 = columns[j], columns[j + 1]
        a, b, c = c0[j:j + 1], c1[j:j + 1], c1[j + 1:j + 2]
        det = a * c - b * b
        inv_a, inv_det = 1.0 / a, 1.0 / det
        pivots = jnp.where(own == j, a, jnp.where(own == j + 1, det * inv_a, pivots))
        below = row > j + 1
        g0 = jnp.where(below, (c0 * c - c1 * b) * inv_det, jnp.where(row == j + 1, b * inv_a, 0.0))
        g1 = jnp.where(below, (c1 * a - c0 * b) * inv_det, 0.0)
        for m in range(j + 2, PANEL):
            columns[m] = columns[m] - g0 * columns[m][j:j + 1] - g1 * columns[m][j + 1:j + 2]
        right = right - wide(g0, width) * right[j:j + 1] - wide(g1, width) * right[j + 1:j + 2]
        left = left - wide(g0, reach) * left[j:j + 1] - wide(g1, reach) * left[j + 1:j + 2]
    scale = lax.rsqrt(pivots)
    done = right[:PANEL] * wide(scale, width), left[:PANEL] * wide(scale, reach)
    return done, right[PANEL:], left[PANEL:]


def invert_factor(gram, inverse):
    n = gram.shape[0]
    for k in range(0, n, WINDOW):
        end = k + WINDOW
        start, reach = k // 128 * 128, -(-end // 128) * 128
        right, left = gram[k:end, start:n], inverse[k:end, :reach]
        done = []
        for first in range(0, WINDOW, PANEL):
            panel, right, left = eliminate_panel(right, left, k - start + first)
            done.append(panel)
        right, left = (jnp.concatenate(part, 0) for part in zip(*done, strict=True))
        inverse[k:end, :reach] = left
        if end < n:
            base = end // 128 * 128
            rest = right[:, base - start:]
            change = transposed_dot(rest, jnp.concatenate([rest, left], 1))[end - base:]
            gram[end:n, base:n] -= change[:, :n - base]
            inverse[end:n, :reach] -= change[:, n - base:]


def basis_kernel(pixels, pix_ref, mine_ref, other_ref, *refs):
    pieces, (basis_ref, gram, inverse) = refs[:-3], refs[-3:]
    n = gram.shape[0]
    half = n // 2
    first = pix_ref[0] == 0
    mine, other = mine_ref[...], other_ref[...]
    above = jnp.where(first, mine[:half], other[:half])
    both = jnp.where(first, other, mine)
    row = lax.broadcasted_iota(jnp.int32, (half, half), 0)
    col = lax.broadcasted_iota(jnp.int32, (half, half), 1)
    eye = row == col
    both, corner = both[:half], both[half:half + 1]
    turned = both.T
    blocks = [jnp.where(row >= col, both, turned), jnp.where(eye, corner, jnp.where(row > col, turned, both))]
    across = [lax.rsqrt(jnp.sum(jnp.where(eye, blk, 0.0), 0, keepdims=True)) for blk in blocks]
    down = [lax.rsqrt(jnp.sum(jnp.where(eye, blk, 0.0), 1, keepdims=True)) for blk in blocks]
    gram[:half, :half] = blocks[0] * across[0] * down[0]
    gram[:half, half:] = above * across[1] * down[0]
    gram[half:, half:] = blocks[1] * across[1] * down[1]
    zero = jnp.zeros((half, half), F32)
    root = math.sqrt(pixels)
    inverse[:half, :half] = jnp.where(eye, jnp.broadcast_to(across[0] * root, (half, half)), 0.0)
    inverse[half:, half:] = jnp.where(eye, jnp.broadcast_to(across[1] * root, (half, half)), 0.0)
    inverse[:half, half:] = zero
    inverse[half:, :half] = zero
    invert_factor(gram, inverse)
    rows = 0
    for x in pieces:
        basis_ref[rows:rows + x.shape[0]] = lax.dot_general(
            x[...], inverse[...], (((1,), (1,)), ((), ())),
            precision=lax.Precision.HIGHEST, preferred_element_type=F32,
        )
        rows += x.shape[0]


def basis_of(pix, mine, other, image, pixels):
    cols = image[0].shape[1]
    rows = sum(x.shape[0] for x in image)
    return pl.pallas_call(
        functools.partial(basis_kernel, pixels),
        in_specs=[SMEM] + [VMEM] * (2 + len(image)),
        out_specs=VMEM,
        out_shape=jax.ShapeDtypeStruct((rows, cols), F32),
        scratch_shapes=[pltpu.VMEM((cols, cols), F32)] * 2,
        compiler_params=params(),
    )(pix, mine, other, *image)


def split(rows):
    ends = [-(-rows // 16 * sum(SHARES[:k]) // sum(SHARES)) * 16 for k in range(len(SHARES) + 1)]
    return [last - first for first, last in zip(ends, ends[1:]) if last > first]


def xor_pairs(n, d):
    return [(i, i ^ d) for i in range(n)]


def on_device(n_bins, spectra, probes):
    rows_dev, bins = spectra.shape
    cols = probes.shape[1]
    rows = rows_dev // n_bins
    me = lax.axis_index("bins")
    pix = lax.axis_index("pix").astype(jnp.int32).reshape(1)
    idx = jnp.stack([me % 2, me // 2]).astype(jnp.int32)

    sizes = split(rows)
    terms = loadings_terms(spectra, probes)
    got = lax.ppermute(terms, "pix", xor_pairs(2, 1))
    outer = n_bins // 2
    blocks = fetch_blocks(idx, spectra, sizes, terms)
    loadings, *parts = image_away(blocks, terms, got, outer)
    n = len(sizes) - 1
    away = [
        lax.ppermute(out.reshape(outer, -1, cols), "bins", xor_pairs(n_bins, 1)) for out in parts[:n]
    ]

    def along_z(sends):
        return [
            lax.ppermute(sends[d - 1], "bins", xor_pairs(n_bins, 2 * d)) for d in range(outer - 1, 0, -1)
        ]

    sides = along_z(parts[n + 1:])
    kept = image_kept(idx, spectra, loadings, rows, sizes[:-1])
    gram = jnp.zeros((cols, cols), F32)
    own, send = sides_chunk(parts[n], sides)
    crossed = lax.ppermute(send, "bins", xor_pairs(n_bins, 1))
    last, gram = gram_chunk(own, [crossed], gram)
    image = []
    for c in range(n):
        first, *sends = add_chunk(idx, away[c], kept[c])
        arrived = along_z(sends)
        if c < n - 1:
            x, gram = gram_chunk(first, arrived, gram)
        else:
            x, mine, other = gram_chunk(first, arrived, gram, pix)
        image.append(x)
    image.append(last)

    mine = mine + lax.ppermute(other, "pix", xor_pairs(2, 1))
    d = 1
    while d < n_bins:
        if d == 1 and n_bins > 2:
            both, near, far = (lax.ppermute(mine, "bins", xor_pairs(n_bins, k)) for k in (3, 1, 2))
            mine, d = (mine + near) + (far + both), 4
        else:
            mine, d = mine + lax.ppermute(mine, "bins", xor_pairs(n_bins, d)), 2 * d
    other = lax.ppermute(mine, "pix", xor_pairs(2, 1))
    basis = basis_of(pix, mine, other, image, 2 * rows_dev)
    return basis.reshape(1, rows, cols)


def solution(mesh):
    return jax.shard_map(
        functools.partial(on_device, mesh.shape["bins"]),
        mesh=mesh,
        in_specs=(P(("parts", "pix"), "bins"), P(("parts", "pix"), None)),
        out_specs=P(("parts", "pix"), "bins", None),
        check_vma=False,
    )
```

```python
import functools
import math
import jax
import jax.numpy as jnp
from jax import lax
from jax.experimental import pallas as pl
from jax.experimental.pallas import tpu as pltpu
from jax.sharding import PartitionSpec as P

SHARES = (13, 12, 7)
PIECES = 8
PANEL = 16
WINDOW = 32
F32 = jnp.float32
BF16 = jnp.bfloat16
MIB = 1 << 20
VMEM = pl.BlockSpec(memory_space=pltpu.VMEM)
SMEM = pl.BlockSpec(memory_space=pltpu.SMEM)
HBM = pl.BlockSpec(memory_space=pltpu.HBM)


def params(mib=32):
    return pltpu.CompilerParams(vmem_limit_bytes=mib * MIB)


def loadings_kernel(spectra_hbm, probes_hbm, terms_ref, spectra_ref, probes_ref, sems):
    rows = spectra_ref.shape[0] // PIECES

    def copies(i):
        part = pl.ds(i * rows, rows)
        return (
            pltpu.make_async_copy(probes_hbm.at[part], probes_ref.at[part], sems.at[0, i]),
            pltpu.make_async_copy(spectra_hbm.at[part], spectra_ref.at[part], sems.at[1, i]),
        )

    for i in range(PIECES):
        for copy in copies(i):
            copy.start()
    for i in range(PIECES):
        for copy in copies(i):
            copy.wait()
        part = pl.ds(i * rows, rows)
        term = lax.dot_general(
            probes_ref[part], spectra_ref[part], (((0,), (0,)), ((), ())), preferred_element_type=F32
        )
        if i == 0:
            terms_ref[...] = term
        else:
            terms_ref[...] += term


def loadings_terms(spectra, probes):
    rows, bins = spectra.shape
    cols = probes.shape[1]
    return pl.pallas_call(
        loadings_kernel,
        in_specs=[HBM, HBM],
        out_specs=VMEM,
        out_shape=jax.ShapeDtypeStruct((cols, bins), F32),
        scratch_shapes=[
            pltpu.VMEM((rows, bins), BF16),
            pltpu.VMEM((rows, cols), BF16),
            pltpu.SemaphoreType.DMA((2, PIECES)),
        ],
        compiler_params=params(51),
        cost_estimate=pl.CostEstimate(
            flops=2 * rows * bins * cols, bytes_accessed=rows * (bins + cols) * 2, transcendentals=0
        ),
    )(spectra, probes)


def block_copies(spectra_hbm, target_ref, sems, sources, size):
    return [
        pltpu.make_async_copy(
            spectra_hbm.at[pl.ds(pl.multiple_of(start, 16), size)], target_ref.at[pl.ds(i * size, size)], sems.at[i]
        )
        for i, start in enumerate(sources)
    ]


def fetch_kernel(sizes, idx_ref, spectra_hbm, after_ref, *refs):
    *targets, sems = refs
    rows, outer = sum(sizes), spectra_hbm.shape[0] // (2 * sum(sizes))
    side, me = idx_ref[0], idx_ref[1]
    copies, first = [], 0
    for c, size in enumerate(sizes):
        if c < len(sizes) - 1:
            sources = [(i * 2 + 1 - side) * rows + first for i in range(outer)]
        else:
            sources = [
                (lax.bitwise_xor(me, d) * 2 + y) * rows + first for d in range(outer) for y in (side, 1 - side)
            ]
        copies += block_copies(spectra_hbm, targets[c], sems.at[c], sources, size)
        first += size
    for copy in copies:
        copy.start()
    for copy in copies:
        copy.wait()


def fetch_blocks(idx, spectra, sizes, after):
    outer, bins = spectra.shape[0] // (2 * sum(sizes)), spectra.shape[1]
    heights = [outer * size for size in sizes[:-1]] + [2 * outer * sizes[-1]]
    return pl.pallas_call(
        functools.partial(fetch_kernel, sizes),
        in_specs=[SMEM, HBM, pl.BlockSpec(memory_space=pl.ANY)],
        out_specs=[VMEM] * len(sizes),
        out_shape=[jax.ShapeDtypeStruct((height, bins), BF16) for height in heights],
        scratch_shapes=[pltpu.SemaphoreType.DMA((len(sizes), 2 * outer))],
        compiler_params=params(46),
        cost_estimate=pl.CostEstimate(flops=0, bytes_accessed=sum(heights) * bins * 4, transcendentals=0),
    )(idx, spectra, after)


def away_kernel(n, *refs):
    blocks, (mine_ref, got_ref, loadings_ref, *outs) = refs[:n], refs[n:]
    loadings_ref[...] = (mine_ref[...] + got_ref[...]).astype(BF16).T
    products = [jnp.dot(x[...], loadings_ref[...], preferred_element_type=F32) for x in blocks]
    for product, out_ref in zip(products[:-1], outs):
        out_ref[...] = product.astype(BF16)
    size = outs[-1].shape[0]
    for d, out_ref in enumerate(outs[n - 1:]):
        out_ref[...] = products[-1][d * size:(d + 1) * size].astype(out_ref.dtype)


def image_away(blocks, mine, got, outer):
    cols, bins = mine.shape
    size = blocks[-1].shape[0] // outer
    shapes = [jax.ShapeDtypeStruct((bins, cols), BF16)]
    shapes += [jax.ShapeDtypeStruct((x.shape[0], cols), BF16) for x in blocks[:-1]]
    shapes += [jax.ShapeDtypeStruct((size, cols), BF16 if d else F32) for d in range(outer)]
    height = sum(x.shape[0] for x in blocks)
    return pl.pallas_call(
        functools.partial(away_kernel, len(blocks)),
        in_specs=[VMEM] * (len(blocks) + 2),
        out_specs=[VMEM] * len(shapes),
        out_shape=shapes,
        compiler_params=params(),
        cost_estimate=pl.CostEstimate(
            flops=2 * height * bins * cols, bytes_accessed=height * cols * 4, transcendentals=0
        ),
    )(*blocks, mine, got)


def kept_kernel(rows, sizes, idx_ref, spectra_hbm, loadings_ref, *refs):
    outs, (blocks_ref, sems) = refs[:-2], refs[-2:]
    outer, size = blocks_ref.shape[0] // sum(sizes), sum(sizes)
    copies = block_copies(
        spectra_hbm, blocks_ref, sems, [(i * 2 + idx_ref[0]) * rows for i in range(outer)], size
    )
    for copy in copies:
        copy.start()
    for i, copy in enumerate(copies):
        copy.wait()
        product = jnp.dot(blocks_ref[i * size:(i + 1) * size], loadings_ref[...], preferred_element_type=F32)
        first = 0
        for out_ref in outs:
            out_ref[i] = product[first:first + out_ref.shape[1]]
            first += out_ref.shape[1]


def image_kept(idx, spectra, loadings, rows, sizes):
    outer, (bins, cols) = spectra.shape[0] // (2 * rows), loadings.shape
    return pl.pallas_call(
        functools.partial(kept_kernel, rows, sizes),
        in_specs=[SMEM, HBM, VMEM],
        out_specs=[VMEM] * len(sizes),
        out_shape=[jax.ShapeDtypeStruct((outer, size, cols), F32) for size in sizes],
        scratch_shapes=[pltpu.VMEM((outer * sum(sizes), bins), BF16), pltpu.SemaphoreType.DMA((outer,))],
        compiler_params=params(48),
        cost_estimate=pl.CostEstimate(
            flops=2 * outer * rows * bins * cols, bytes_accessed=outer * rows * (bins * 2 + cols * 4), transcendentals=0
        ),
    )(idx, spectra, loadings)


def sides_kernel(mine_ref, *refs):
    *got_refs, own_ref, send_ref = refs
    total = mine_ref[...]
    for got in got_refs:
        total = total + got[...].astype(F32)
    size = own_ref.shape[0]
    own_ref[...] = total[:size]
    send_ref[...] = total[size:].astype(BF16)


def sides_chunk(mine, got):
    size, cols = mine.shape[0] // 2, mine.shape[1]
    return pl.pallas_call(
        sides_kernel,
        in_specs=[VMEM] * (1 + len(got)),
        out_specs=[VMEM] * 2,
        out_shape=[jax.ShapeDtypeStruct((size, cols), F32), jax.ShapeDtypeStruct((size, cols), BF16)],
        compiler_params=params(),
        cost_estimate=pl.CostEstimate(flops=8 * size * cols, bytes_accessed=16 * size * cols, transcendentals=0),
    )(mine, *got)


def add_kernel(idx_ref, got_ref, kept_ref, own_ref, *send_refs):
    me = idx_ref[1]
    own_ref[...] = got_ref[me].astype(F32) + kept_ref[me]
    for d, send in enumerate(send_refs):
        other = lax.bitwise_xor(me, d + 1)
        send[...] = (got_ref[other].astype(F32) + kept_ref[other]).astype(send.dtype)


def add_chunk(idx, got, kept):
    outer, piece, cols = got.shape
    return pl.pallas_call(
        add_kernel,
        in_specs=[SMEM, VMEM, VMEM],
        out_specs=[VMEM] * outer,
        out_shape=[jax.ShapeDtypeStruct((piece, cols), F32)]
        + [jax.ShapeDtypeStruct((piece, cols), BF16)] * (outer - 1),
        compiler_params=params(),
        cost_estimate=pl.CostEstimate(
            flops=outer * piece * cols, bytes_accessed=outer * piece * cols * 8, transcendentals=0
        ),
    )(idx, got, kept)


def gram_kernel(n, last, *refs):
    if last:
        pix_ref, refs = refs[0], refs[1:]
    own_ref, got, (gram_in, x_ref, *out) = refs[0], refs[1:n], refs[n:]
    x = own_ref[...]
    for g in got:
        x = x + g[...].astype(F32)
    x_ref[...] = x
    gram = gram_in[...] + lax.dot_general(
        x, x, (((0,), (0,)), ((), ())), precision=lax.Precision.HIGHEST, preferred_element_type=F32
    )
    if not last:
        out[0][...] = gram
        return
    half = gram.shape[0] // 2
    mine, other = out
    row = lax.broadcasted_iota(jnp.int32, (half, half), 0)
    col = lax.broadcasted_iota(jnp.int32, (half, half), 1)
    corner = gram[half:, half:]
    diag = jnp.sum(jnp.where(row == col, corner, 0.0), 0, keepdims=True)
    above = gram[:half, half:]
    both = jnp.where(row >= col, gram[:half, :half], corner)
    first = pix_ref[0] == 0
    mine[:half] = jnp.where(first, above, both)
    other[:half] = jnp.where(first, both, above)
    mine[half:] = jnp.broadcast_to(diag, (8, half))
    other[half:] = jnp.broadcast_to(diag, (8, half))


def gram_chunk(own, got, gram, pix=None):
    piece, cols = own.shape
    n = 1 + len(got)
    half = cols // 2
    last = pix is not None
    shapes = [(half + 8, half)] * 2 if last else [(cols, cols)]
    return pl.pallas_call(
        functools.partial(gram_kernel, n, last),
        in_specs=[SMEM] * last + [VMEM] * (n + 1),
        out_specs=[VMEM] * (1 + len(shapes)),
        out_shape=[jax.ShapeDtypeStruct(s, F32) for s in [(piece, cols)] + shapes],
        compiler_params=params(),
        cost_estimate=pl.CostEstimate(
            flops=12 * piece * cols * cols, bytes_accessed=n * piece * cols * 4, transcendentals=0
        ),
    )(*[pix] * last, own, *got, gram)


def stacked_terms(a, b):
    def terms(x):
        high = x.astype(BF16)
        rest = x - high.astype(F32)
        middle = rest.astype(BF16)
        return high, middle, (rest - middle.astype(F32)).astype(BF16)

    (a0, a1, a2), (b0, b1, b2) = terms(a), terms(b)
    return jnp.concatenate([a0, a0, a1, a1, a0, a2], 0).T, jnp.concatenate([b0, b1, b0, b1, b2, b0], 0)


def wide(column, width):
    return column if width == 128 else jnp.concatenate([column] * (width // 128), 1)


def eliminate_panel(right, left, at):
    rows, width = right.shape
    reach = left.shape[1]
    row = lax.broadcasted_iota(jnp.int32, (rows, 128), 0)
    own = row[:PANEL]
    columns = [jnp.broadcast_to(right[:, at + j:at + j + 1], (rows, 128)) for j in range(PANEL)]
    pivots = jnp.ones((PANEL, 128), F32)
    for j in range(0, PANEL, 2):
        c0, c1 = columns[j], columns[j + 1]
        a, b, c = c0[j:j + 1], c1[j:j + 1], c1[j + 1:j + 2]
        det = a * c - b * b
        inv_a, inv_det = 1.0 / a, 1.0 / det
        pivots = jnp.where(own == j, a, jnp.where(own == j + 1, det * inv_a, pivots))
        below = row > j + 1
        g0 = jnp.where(below, (c0 * c - c1 * b) * inv_det, jnp.where(row == j + 1, b * inv_a, 0.0))
        g1 = jnp.where(below, (c1 * a - c0 * b) * inv_det, 0.0)
        for m in range(j + 2, PANEL):
            columns[m] = columns[m] - g0 * columns[m][j:j + 1] - g1 * columns[m][j + 1:j + 2]
        right = right - wide(g0, width) * right[j:j + 1] - wide(g1, width) * right[j + 1:j + 2]
        left = left - wide(g0, reach) * left[j:j + 1] - wide(g1, reach) * left[j + 1:j + 2]
    scale = lax.rsqrt(pivots)
    done = right[:PANEL] * wide(scale, width), left[:PANEL] * wide(scale, reach)
    return done, right[PANEL:], left[PANEL:]


def invert_factor(gram, inverse):
    n = gram.shape[0]
    for k in range(0, n, WINDOW):
        end = k + WINDOW
        start, reach = k // 128 * 128, -(-end // 128) * 128
        right, left = gram[k:end, start:n], inverse[k:end, :reach]
        done = []
        for first in range(0, WINDOW, PANEL):
            panel, right, left = eliminate_panel(right, left, k - start + first)
            done.append(panel)
        right, left = (jnp.concatenate(part, 0) for part in zip(*done, strict=True))
        inverse[k:end, :reach] = left
        if end < n:
            base = end // 128 * 128
            rest = right[:, base - start:]
            turned, stacked = stacked_terms(rest, jnp.concatenate([rest, left], 1))
            cuts = [end, min(end + WINDOW, n), n]
            for low, high in zip(cuts, cuts[1:]):
                if high > low:
                    change = jnp.dot(turned[low - base:high - base], stacked, preferred_element_type=F32)
                    gram[low:high, base:n] -= change[:, :n - base]
                    inverse[low:high, :reach] -= change[:, n - base:]


def basis_kernel(pixels, pix_ref, mine_ref, other_ref, *refs):
    pieces, (basis_ref, gram, inverse) = refs[:-3], refs[-3:]
    n = gram.shape[0]
    half = n // 2
    first = pix_ref[0] == 0
    mine, other = mine_ref[...], other_ref[...]
    above = jnp.where(first, mine[:half], other[:half])
    both = jnp.where(first, other, mine)
    row = lax.broadcasted_iota(jnp.int32, (half, half), 0)
    col = lax.broadcasted_iota(jnp.int32, (half, half), 1)
    eye = row == col
    both, corner = both[:half], both[half:half + 1]
    turned = both.T
    blocks = [jnp.where(row >= col, both, turned), jnp.where(eye, corner, jnp.where(row > col, turned, both))]
    across = [lax.rsqrt(jnp.sum(jnp.where(eye, blk, 0.0), 0, keepdims=True)) for blk in blocks]
    down = [lax.rsqrt(jnp.sum(jnp.where(eye, blk, 0.0), 1, keepdims=True)) for blk in blocks]
    gram[:half, :half] = blocks[0] * across[0] * down[0]
    gram[:half, half:] = above * across[1] * down[0]
    gram[half:, half:] = blocks[1] * across[1] * down[1]
    zero = jnp.zeros((half, half), F32)
    root = math.sqrt(pixels)
    inverse[:half, :half] = jnp.where(eye, jnp.broadcast_to(across[0] * root, (half, half)), 0.0)
    inverse[half:, half:] = jnp.where(eye, jnp.broadcast_to(across[1] * root, (half, half)), 0.0)
    inverse[:half, half:] = zero
    inverse[half:, :half] = zero
    invert_factor(gram, inverse)
    rows = 0
    for x in pieces:
        basis_ref[rows:rows + x.shape[0]] = lax.dot_general(
            x[...], inverse[...], (((1,), (1,)), ((), ())),
            precision=lax.Precision.HIGHEST, preferred_element_type=F32,
        )
        rows += x.shape[0]


def basis_of(pix, mine, other, image, pixels):
    cols = image[0].shape[1]
    rows = sum(x.shape[0] for x in image)
    return pl.pallas_call(
        functools.partial(basis_kernel, pixels),
        in_specs=[SMEM] + [VMEM] * (2 + len(image)),
        out_specs=VMEM,
        out_shape=jax.ShapeDtypeStruct((rows, cols), F32),
        scratch_shapes=[pltpu.VMEM((cols, cols), F32)] * 2,
        compiler_params=params(),
    )(pix, mine, other, *image)


def split(rows):
    ends = [-(-rows // 16 * sum(SHARES[:k]) // sum(SHARES)) * 16 for k in range(len(SHARES) + 1)]
    return [last - first for first, last in zip(ends, ends[1:]) if last > first]


def xor_pairs(n, d):
    return [(i, i ^ d) for i in range(n)]


def on_device(n_bins, spectra, probes):
    rows_dev, bins = spectra.shape
    cols = probes.shape[1]
    rows = rows_dev // n_bins
    me = lax.axis_index("bins")
    pix = lax.axis_index("pix").astype(jnp.int32).reshape(1)
    idx = jnp.stack([me % 2, me // 2]).astype(jnp.int32)

    sizes = split(rows)
    terms = loadings_terms(spectra, probes)
    got = lax.ppermute(terms, "pix", xor_pairs(2, 1))
    outer = n_bins // 2
    blocks = fetch_blocks(idx, spectra, sizes, terms)
    loadings, *parts = image_away(blocks, terms, got, outer)
    n = len(sizes) - 1
    away = [
        lax.ppermute(out.reshape(outer, -1, cols), "bins", xor_pairs(n_bins, 1)) for out in parts[:n]
    ]

    def along_z(sends):
        return [
            lax.ppermute(sends[d - 1], "bins", xor_pairs(n_bins, 2 * d)) for d in range(outer - 1, 0, -1)
        ]

    sides = along_z(parts[n + 1:])
    kept = image_kept(idx, spectra, loadings, rows, sizes[:-1])
    gram = jnp.zeros((cols, cols), F32)
    own, send = sides_chunk(parts[n], sides)
    crossed = lax.ppermute(send, "bins", xor_pairs(n_bins, 1))
    last, gram = gram_chunk(own, [crossed], gram)
    image = []
    for c in range(n):
        first, *sends = add_chunk(idx, away[c], kept[c])
        arrived = along_z(sends)
        if c < n - 1:
            x, gram = gram_chunk(first, arrived, gram)
        else:
            x, mine, other = gram_chunk(first, arrived, gram, pix)
        image.append(x)
    image.append(last)

    mine = mine + lax.ppermute(other, "pix", xor_pairs(2, 1))
    d = 1
    while d < n_bins:
        if d == 1 and n_bins > 2:
            both, near, far = (lax.ppermute(mine, "bins", xor_pairs(n_bins, k)) for k in (3, 1, 2))
            mine, d = (mine + near) + (far + both), 4
        else:
            mine, d = mine + lax.ppermute(mine, "bins", xor_pairs(n_bins, d)), 2 * d
    other = lax.ppermute(mine, "pix", xor_pairs(2, 1))
    basis = basis_of(pix, mine, other, image, 2 * rows_dev)
    return basis.reshape(1, rows, cols)


def solution(mesh):
    return jax.shard_map(
        functools.partial(on_device, mesh.shape["bins"]),
        mesh=mesh,
        in_specs=(P(("parts", "pix"), "bins"), P(("parts", "pix"), None)),
        out_specs=P(("parts", "pix"), "bins", None),
        check_vma=False,
    )
```

```python
import functools
import math
import jax
import jax.numpy as jnp
from jax import lax
from jax.experimental import pallas as pl
from jax.experimental.pallas import tpu as pltpu
from jax.sharding import PartitionSpec as P

SHARES = (13, 12, 7)
PIECES = 8
PANEL = 16
WINDOW = 32
F32 = jnp.float32
BF16 = jnp.bfloat16
MIB = 1 << 20
VMEM = pl.BlockSpec(memory_space=pltpu.VMEM)
SMEM = pl.BlockSpec(memory_space=pltpu.SMEM)
HBM = pl.BlockSpec(memory_space=pltpu.HBM)


def params(mib=32):
    return pltpu.CompilerParams(vmem_limit_bytes=mib * MIB)


def loadings_kernel(spectra_hbm, probes_hbm, terms_ref, spectra_ref, probes_ref, sems):
    rows = spectra_ref.shape[0] // PIECES

    def copies(i):
        part = pl.ds(i * rows, rows)
        return (
            pltpu.make_async_copy(probes_hbm.at[part], probes_ref.at[part], sems.at[0, i]),
            pltpu.make_async_copy(spectra_hbm.at[part], spectra_ref.at[part], sems.at[1, i]),
        )

    for i in range(PIECES):
        for copy in copies(i):
            copy.start()
    for i in range(PIECES):
        for copy in copies(i):
            copy.wait()
        part = pl.ds(i * rows, rows)
        term = lax.dot_general(
            probes_ref[part], spectra_ref[part], (((0,), (0,)), ((), ())), preferred_element_type=F32
        )
        if i == 0:
            terms_ref[...] = term
        else:
            terms_ref[...] += term


def loadings_terms(spectra, probes):
    rows, bins = spectra.shape
    cols = probes.shape[1]
    return pl.pallas_call(
        loadings_kernel,
        in_specs=[HBM, HBM],
        out_specs=VMEM,
        out_shape=jax.ShapeDtypeStruct((cols, bins), F32),
        scratch_shapes=[
            pltpu.VMEM((rows, bins), BF16),
            pltpu.VMEM((rows, cols), BF16),
            pltpu.SemaphoreType.DMA((2, PIECES)),
        ],
        compiler_params=params(51),
        cost_estimate=pl.CostEstimate(
            flops=2 * rows * bins * cols, bytes_accessed=rows * (bins + cols) * 2, transcendentals=0
        ),
    )(spectra, probes)


def block_copies(spectra_hbm, target_ref, sems, sources, size):
    return [
        pltpu.make_async_copy(
            spectra_hbm.at[pl.ds(pl.multiple_of(start, 16), size)], target_ref.at[pl.ds(i * size, size)], sems.at[i]
        )
        for i, start in enumerate(sources)
    ]


def fetch_kernel(sizes, idx_ref, spectra_hbm, after_ref, *refs):
    *targets, sems = refs
    rows, outer = sum(sizes), spectra_hbm.shape[0] // (2 * sum(sizes))
    side, me = idx_ref[0], idx_ref[1]
    copies, first = [], 0
    for c, size in enumerate(sizes):
        if c < len(sizes) - 1:
            sources = [(i * 2 + 1 - side) * rows + first for i in range(outer)]
        else:
            sources = [
                (lax.bitwise_xor(me, d) * 2 + y) * rows + first for d in range(outer) for y in (side, 1 - side)
            ]
        copies += block_copies(spectra_hbm, targets[c], sems.at[c], sources, size)
        first += size
    for copy in copies:
        copy.start()
    for copy in copies:
        copy.wait()


def fetch_blocks(idx, spectra, sizes, after):
    outer, bins = spectra.shape[0] // (2 * sum(sizes)), spectra.shape[1]
    heights = [outer * size for size in sizes[:-1]] + [2 * outer * sizes[-1]]
    return pl.pallas_call(
        functools.partial(fetch_kernel, sizes),
        in_specs=[SMEM, HBM, pl.BlockSpec(memory_space=pl.ANY)],
        out_specs=[VMEM] * len(sizes),
        out_shape=[jax.ShapeDtypeStruct((height, bins), BF16) for height in heights],
        scratch_shapes=[pltpu.SemaphoreType.DMA((len(sizes), 2 * outer))],
        compiler_params=params(46),
        cost_estimate=pl.CostEstimate(flops=0, bytes_accessed=sum(heights) * bins * 4, transcendentals=0),
    )(idx, spectra, after)


def away_kernel(n, *refs):
    blocks, (mine_ref, got_ref, loadings_ref, *outs) = refs[:n], refs[n:]
    loadings_ref[...] = (mine_ref[...] + got_ref[...]).astype(BF16).T
    products = [jnp.dot(x[...], loadings_ref[...], preferred_element_type=F32) for x in blocks]
    for product, out_ref in zip(products[:-1], outs):
        out_ref[...] = product.astype(BF16)
    size = outs[-1].shape[0]
    for d, out_ref in enumerate(outs[n - 1:]):
        out_ref[...] = products[-1][d * size:(d + 1) * size].astype(out_ref.dtype)


def image_away(blocks, mine, got, outer):
    cols, bins = mine.shape
    size = blocks[-1].shape[0] // outer
    shapes = [jax.ShapeDtypeStruct((bins, cols), BF16)]
    shapes += [jax.ShapeDtypeStruct((x.shape[0], cols), BF16) for x in blocks[:-1]]
    shapes += [jax.ShapeDtypeStruct((size, cols), BF16 if d else F32) for d in range(outer)]
    height = sum(x.shape[0] for x in blocks)
    return pl.pallas_call(
        functools.partial(away_kernel, len(blocks)),
        in_specs=[VMEM] * (len(blocks) + 2),
        out_specs=[VMEM] * len(shapes),
        out_shape=shapes,
        compiler_params=params(),
        cost_estimate=pl.CostEstimate(
            flops=2 * height * bins * cols, bytes_accessed=height * cols * 4, transcendentals=0
        ),
    )(*blocks, mine, got)


def kept_kernel(rows, sizes, idx_ref, spectra_hbm, loadings_ref, *refs):
    outs, (blocks_ref, sems) = refs[:-2], refs[-2:]
    outer, size = blocks_ref.shape[0] // sum(sizes), sum(sizes)
    copies = block_copies(
        spectra_hbm, blocks_ref, sems, [(i * 2 + idx_ref[0]) * rows for i in range(outer)], size
    )
    for copy in copies:
        copy.start()
    for i, copy in enumerate(copies):
        copy.wait()
        product = jnp.dot(blocks_ref[i * size:(i + 1) * size], loadings_ref[...], preferred_element_type=F32)
        first = 0
        for out_ref in outs:
            out_ref[i] = product[first:first + out_ref.shape[1]]
            first += out_ref.shape[1]


def image_kept(idx, spectra, loadings, rows, sizes):
    outer, (bins, cols) = spectra.shape[0] // (2 * rows), loadings.shape
    return pl.pallas_call(
        functools.partial(kept_kernel, rows, sizes),
        in_specs=[SMEM, HBM, VMEM],
        out_specs=[VMEM] * len(sizes),
        out_shape=[jax.ShapeDtypeStruct((outer, size, cols), F32) for size in sizes],
        scratch_shapes=[pltpu.VMEM((outer * sum(sizes), bins), BF16), pltpu.SemaphoreType.DMA((outer,))],
        compiler_params=params(48),
        cost_estimate=pl.CostEstimate(
            flops=2 * outer * rows * bins * cols, bytes_accessed=outer * rows * (bins * 2 + cols * 4), transcendentals=0
        ),
    )(idx, spectra, loadings)


def sides_kernel(mine_ref, *refs):
    *got_refs, own_ref, send_ref = refs
    total = mine_ref[...]
    for got in got_refs:
        total = total + got[...].astype(F32)
    size = own_ref.shape[0]
    own_ref[...] = total[:size]
    send_ref[...] = total[size:].astype(BF16)


def sides_chunk(mine, got):
    size, cols = mine.shape[0] // 2, mine.shape[1]
    return pl.pallas_call(
        sides_kernel,
        in_specs=[VMEM] * (1 + len(got)),
        out_specs=[VMEM] * 2,
        out_shape=[jax.ShapeDtypeStruct((size, cols), F32), jax.ShapeDtypeStruct((size, cols), BF16)],
        compiler_params=params(),
        cost_estimate=pl.CostEstimate(flops=8 * size * cols, bytes_accessed=16 * size * cols, transcendentals=0),
    )(mine, *got)


def add_kernel(idx_ref, got_ref, kept_ref, own_ref, *send_refs):
    me = idx_ref[1]
    own_ref[...] = got_ref[me].astype(F32) + kept_ref[me]
    for d, send in enumerate(send_refs):
        other = lax.bitwise_xor(me, d + 1)
        send[...] = (got_ref[other].astype(F32) + kept_ref[other]).astype(send.dtype)


def add_chunk(idx, got, kept):
    outer, piece, cols = got.shape
    return pl.pallas_call(
        add_kernel,
        in_specs=[SMEM, VMEM, VMEM],
        out_specs=[VMEM] * outer,
        out_shape=[jax.ShapeDtypeStruct((piece, cols), F32)]
        + [jax.ShapeDtypeStruct((piece, cols), BF16)] * (outer - 1),
        compiler_params=params(),
        cost_estimate=pl.CostEstimate(
            flops=outer * piece * cols, bytes_accessed=outer * piece * cols * 8, transcendentals=0
        ),
    )(idx, got, kept)


def gram_kernel(n, last, *refs):
    if last:
        pix_ref, refs = refs[0], refs[1:]
    own_ref, got, (gram_in, x_ref, *out) = refs[0], refs[1:n], refs[n:]
    x = own_ref[...]
    for g in got:
        x = x + g[...].astype(F32)
    x_ref[...] = x
    gram = gram_in[...] + jnp.dot(*stacked_terms(x, x), preferred_element_type=F32)
    if not last:
        out[0][...] = gram
        return
    half = gram.shape[0] // 2
    mine, other = out
    row = lax.broadcasted_iota(jnp.int32, (half, half), 0)
    col = lax.broadcasted_iota(jnp.int32, (half, half), 1)
    corner = gram[half:, half:]
    diag = jnp.sum(jnp.where(row == col, corner, 0.0), 0, keepdims=True)
    above = gram[:half, half:]
    both = jnp.where(row >= col, gram[:half, :half], corner)
    first = pix_ref[0] == 0
    mine[:half] = jnp.where(first, above, both)
    other[:half] = jnp.where(first, both, above)
    mine[half:] = jnp.broadcast_to(diag, (8, half))
    other[half:] = jnp.broadcast_to(diag, (8, half))


def gram_chunk(own, got, gram, pix=None):
    piece, cols = own.shape
    n = 1 + len(got)
    half = cols // 2
    last = pix is not None
    shapes = [(half + 8, half)] * 2 if last else [(cols, cols)]
    return pl.pallas_call(
        functools.partial(gram_kernel, n, last),
        in_specs=[SMEM] * last + [VMEM] * (n + 1),
        out_specs=[VMEM] * (1 + len(shapes)),
        out_shape=[jax.ShapeDtypeStruct(s, F32) for s in [(piece, cols)] + shapes],
        compiler_params=params(),
        cost_estimate=pl.CostEstimate(
            flops=12 * piece * cols * cols, bytes_accessed=n * piece * cols * 4, transcendentals=0
        ),
    )(*[pix] * last, own, *got, gram)


def stacked_terms(a, b):
    def terms(x):
        high = x.astype(BF16)
        rest = x - high.astype(F32)
        middle = rest.astype(BF16)
        return high, middle, (rest - middle.astype(F32)).astype(BF16)

    (a0, a1, a2), (b0, b1, b2) = terms(a), terms(b)
    return jnp.concatenate([a0, a0, a1, a1, a0, a2], 0).T, jnp.concatenate([b0, b1, b0, b1, b2, b0], 0)


def wide(column, width):
    return column if width == 128 else jnp.concatenate([column] * (width // 128), 1)


def eliminate_panel(right, left, at):
    rows, width = right.shape
    reach = left.shape[1]
    row = lax.broadcasted_iota(jnp.int32, (rows, 128), 0)
    own = row[:PANEL]
    columns = [jnp.broadcast_to(right[:, at + j:at + j + 1], (rows, 128)) for j in range(PANEL)]
    pivots = jnp.ones((PANEL, 128), F32)
    for j in range(0, PANEL, 2):
        c0, c1 = columns[j], columns[j + 1]
        a, b, c = c0[j:j + 1], c1[j:j + 1], c1[j + 1:j + 2]
        det = a * c - b * b
        inv_a, inv_det = 1.0 / a, 1.0 / det
        pivots = jnp.where(own == j, a, jnp.where(own == j + 1, det * inv_a, pivots))
        below = row > j + 1
        g0 = jnp.where(below, (c0 * c - c1 * b) * inv_det, jnp.where(row == j + 1, b * inv_a, 0.0))
        g1 = jnp.where(below, (c1 * a - c0 * b) * inv_det, 0.0)
        for m in range(j + 2, PANEL):
            columns[m] = columns[m] - g0 * columns[m][j:j + 1] - g1 * columns[m][j + 1:j + 2]
        right = right - wide(g0, width) * right[j:j + 1] - wide(g1, width) * right[j + 1:j + 2]
        left = left - wide(g0, reach) * left[j:j + 1] - wide(g1, reach) * left[j + 1:j + 2]
    scale = lax.rsqrt(pivots)
    done = right[:PANEL] * wide(scale, width), left[:PANEL] * wide(scale, reach)
    return done, right[PANEL:], left[PANEL:]


def invert_factor(gram, inverse):
    n = gram.shape[0]
    for k in range(0, n, WINDOW):
        end = k + WINDOW
        start, reach = k // 128 * 128, -(-end // 128) * 128
        right, left = gram[k:end, start:n], inverse[k:end, :reach]
        done = []
        for first in range(0, WINDOW, PANEL):
            panel, right, left = eliminate_panel(right, left, k - start + first)
            done.append(panel)
        right, left = (jnp.concatenate(part, 0) for part in zip(*done, strict=True))
        inverse[k:end, :reach] = left
        if end < n:
            base = end // 128 * 128
            rest = right[:, base - start:]
            turned, stacked = stacked_terms(rest, jnp.concatenate([rest, left], 1))
            cuts = [end, min(end + WINDOW, n), n]
            for low, high in zip(cuts, cuts[1:]):
                if high > low:
                    change = jnp.dot(turned[low - base:high - base], stacked, preferred_element_type=F32)
                    gram[low:high, base:n] -= change[:, :n - base]
                    inverse[low:high, :reach] -= change[:, n - base:]


def basis_kernel(pixels, pix_ref, mine_ref, other_ref, *refs):
    pieces, (basis_ref, gram, inverse) = refs[:-3], refs[-3:]
    n = gram.shape[0]
    half = n // 2
    first = pix_ref[0] == 0
    mine, other = mine_ref[...], other_ref[...]
    above = jnp.where(first, mine[:half], other[:half])
    both = jnp.where(first, other, mine)
    row = lax.broadcasted_iota(jnp.int32, (half, half), 0)
    col = lax.broadcasted_iota(jnp.int32, (half, half), 1)
    eye = row == col
    both, corner = both[:half], both[half:half + 1]
    turned = both.T
    blocks = [jnp.where(row >= col, both, turned), jnp.where(eye, corner, jnp.where(row > col, turned, both))]
    across = [lax.rsqrt(jnp.sum(jnp.where(eye, blk, 0.0), 0, keepdims=True)) for blk in blocks]
    down = [lax.rsqrt(jnp.sum(jnp.where(eye, blk, 0.0), 1, keepdims=True)) for blk in blocks]
    gram[:half, :half] = blocks[0] * across[0] * down[0]
    gram[:half, half:] = above * across[1] * down[0]
    gram[half:, half:] = blocks[1] * across[1] * down[1]
    zero = jnp.zeros((half, half), F32)
    root = math.sqrt(pixels)
    inverse[:half, :half] = jnp.where(eye, jnp.broadcast_to(across[0] * root, (half, half)), 0.0)
    inverse[half:, half:] = jnp.where(eye, jnp.broadcast_to(across[1] * root, (half, half)), 0.0)
    inverse[:half, half:] = zero
    inverse[half:, :half] = zero
    invert_factor(gram, inverse)
    rows = 0
    for x in pieces:
        basis_ref[rows:rows + x.shape[0]] = lax.dot_general(
            x[...], inverse[...], (((1,), (1,)), ((), ())),
            precision=lax.Precision.HIGHEST, preferred_element_type=F32,
        )
        rows += x.shape[0]


def basis_of(pix, mine, other, image, pixels):
    cols = image[0].shape[1]
    rows = sum(x.shape[0] for x in image)
    return pl.pallas_call(
        functools.partial(basis_kernel, pixels),
        in_specs=[SMEM] + [VMEM] * (2 + len(image)),
        out_specs=VMEM,
        out_shape=jax.ShapeDtypeStruct((rows, cols), F32),
        scratch_shapes=[pltpu.VMEM((cols, cols), F32)] * 2,
        compiler_params=params(),
    )(pix, mine, other, *image)


def split(rows):
    ends = [-(-rows // 16 * sum(SHARES[:k]) // sum(SHARES)) * 16 for k in range(len(SHARES) + 1)]
    return [last - first for first, last in zip(ends, ends[1:]) if last > first]


def xor_pairs(n, d):
    return [(i, i ^ d) for i in range(n)]


def on_device(n_bins, spectra, probes):
    rows_dev, bins = spectra.shape
    cols = probes.shape[1]
    rows = rows_dev // n_bins
    me = lax.axis_index("bins")
    pix = lax.axis_index("pix").astype(jnp.int32).reshape(1)
    idx = jnp.stack([me % 2, me // 2]).astype(jnp.int32)

    sizes = split(rows)
    terms = loadings_terms(spectra, probes)
    got = lax.ppermute(terms, "pix", xor_pairs(2, 1))
    outer = n_bins // 2
    blocks = fetch_blocks(idx, spectra, sizes, terms)
    loadings, *parts = image_away(blocks, terms, got, outer)
    n = len(sizes) - 1
    away = [
        lax.ppermute(out.reshape(outer, -1, cols), "bins", xor_pairs(n_bins, 1)) for out in parts[:n]
    ]

    def along_z(sends):
        return [
            lax.ppermute(sends[d - 1], "bins", xor_pairs(n_bins, 2 * d)) for d in range(outer - 1, 0, -1)
        ]

    sides = along_z(parts[n + 1:])
    kept = image_kept(idx, spectra, loadings, rows, sizes[:-1])
    gram = jnp.zeros((cols, cols), F32)
    own, send = sides_chunk(parts[n], sides)
    crossed = lax.ppermute(send, "bins", xor_pairs(n_bins, 1))
    last, gram = gram_chunk(own, [crossed], gram)
    image = []
    for c in range(n):
        first, *sends = add_chunk(idx, away[c], kept[c])
        arrived = along_z(sends)
        if c < n - 1:
            x, gram = gram_chunk(first, arrived, gram)
        else:
            x, mine, other = gram_chunk(first, arrived, gram, pix)
        image.append(x)
    image.append(last)

    mine = mine + lax.ppermute(other, "pix", xor_pairs(2, 1))
    d = 1
    while d < n_bins:
        if d == 1 and n_bins > 2:
            both, near, far = (lax.ppermute(mine, "bins", xor_pairs(n_bins, k)) for k in (3, 1, 2))
            mine, d = (mine + near) + (far + both), 4
        else:
            mine, d = mine + lax.ppermute(mine, "bins", xor_pairs(n_bins, d)), 2 * d
    other = lax.ppermute(mine, "pix", xor_pairs(2, 1))
    basis = basis_of(pix, mine, other, image, 2 * rows_dev)
    return basis.reshape(1, rows, cols)


def solution(mesh):
    return jax.shard_map(
        functools.partial(on_device, mesh.shape["bins"]),
        mesh=mesh,
        in_specs=(P(("parts", "pix"), "bins"), P(("parts", "pix"), None)),
        out_specs=P(("parts", "pix"), "bins", None),
        check_vma=False,
    )
```
